256 devices in a mesh: rad: 4 (over y), ma: 64 (over x, z, core).
Axes of the slice: x: 4, y: 4, z: 8, core: 2. Of those that a mesh axis runs over, the one named last changes fastest.
Arguments:
- velocity: bfloat16 [4, 3, 2, 1024, 1536], P('rad', None, None, 'ma'), may hold values from -0.1875 to 0.1875
- test_fields: bfloat16 [4, 2, 3, 2, 1024, 1536], P('rad', None, None, None, 'ma'), may hold values from -0.1875 to 0.1875
- order_slots: int32 [1024], replicated, may hold values from 0 to 1023, as said below
Outputs:
- emf_out: bfloat16 [4, 2, 3, 2, 1024, 1536], P('rad', None, None, None, 'ma')
- emf_deriv: bfloat16 [4, 2, 3, 2, 1024, 1536], P('rad', None, None, None, 'ma')
The draws below stay inside these ranges and needn't reach their ends.
Inputs may be any that keep to these rules, and one draw needn't show every extreme that they name: `order_slots`: every order from 0 to 1023 stands in exactly one slot, and slots 2i and 2i + 1 hold two orders that sum to 1023.
All inputs are finite; a program needn't handle non-finite values.
Results may differ from the reference program's by a relative error of at most 0.0064.
Values may be sent and summed in bfloat16 or wider, within the bound.
A program may use at most 128 MiB of HBM per device.

```python
import math
import jax
import jax.numpy as jnp
import numpy as np
from jax import lax

M = 1024
NTH = 1536
NPHI = 3072
NR = 4


def draw_order_slots(key, part):
    half_count = M // 2
    pair_ids = jax.random.permutation(jax.random.fold_in(key, 11), half_count).astype(jnp.int32)
    flip_bits = jax.random.randint(jax.random.fold_in(key, 12), (half_count,), 0, 2).astype(jnp.int32)
    first_order = jnp.where(flip_bits == 1, M - 1 - pair_ids, pair_ids)
    second_order = M - 1 - first_order
    return jnp.stack([first_order, second_order], axis=1).reshape(M).astype(jnp.int32)


def shard_levels(own_key, extent, split, low, top_value):
    def one(position, blocks):
        draws = jax.random.uniform(jax.random.fold_in(jax.random.fold_in(own_key, 6), position), (blocks,), jnp.float32, low / len(split), top_value / len(split))
        return jnp.repeat(jnp.exp(draws), extent[position] // blocks).reshape((-1,) + (1,) * (len(extent) - position - 1))

    level = one(*split[0])
    for cut in split[1:]:
        level = level * one(*cut)
    return level


def centred(own_key, dims, width, bound, cuts=(), held_as=jnp.bfloat16):
    factor_of = shard_levels(own_key, dims, cuts, -0.22, 0.18) if cuts else 1.0
    result = jax.random.normal(own_key, dims, jnp.float32) * width * factor_of
    return jnp.minimum(jnp.maximum(result, -bound), bound).astype(held_as)


def setup_inputs(seed: int = 0) -> dict:
    key_list = jax.random.split(jax.random.key(seed), 4)
    return {
        "velocity": centred(key_list[0], (NR, 3, 2, M, NTH), M ** -0.5, 0.1875, ((0, 4), (3, 64))),
        "test_fields": centred(key_list[1], (NR, 2, 3, 2, M, NTH), M ** -0.5, 0.1875, ((0, 4), (4, 64))),
        "order_slots": draw_order_slots(jax.random.fold_in(key_list[3], 71), 0),
    }


def live_mask(orders, cycle_ids, total_orders, total_cycles):
    nearest = jnp.minimum(cycle_ids + 1, total_cycles - cycle_ids)
    return orders[:, None] * total_cycles <= 2 * total_orders * nearest[None, :]


def phase_table(orders, first_lon, lon_count, lon_total):
    longitudes = first_lon + jnp.arange(lon_count, dtype=jnp.int32)
    phase_int = (orders[:, None] * longitudes[None, :]) % lon_total
    angles = phase_int.astype(jnp.float32) * (2.0 * math.pi / lon_total)
    return jnp.stack([jnp.cos(angles), -jnp.sin(angles)]).astype(jnp.bfloat16)


def cheb_matrix(level_count):
    levels_at = np.arange(level_count)
    points = np.cos(np.pi * levels_at / (level_count - 1))
    weights = np.where((levels_at == 0) | (levels_at == level_count - 1), 2.0, 1.0) * np.where(levels_at % 2 == 0, 1.0, -1.0)
    identity = np.eye(level_count)
    spread = points[:, None] - points[None, :] + identity
    offdiag = (weights[:, None] / weights[None, :]) / spread * (1.0 - identity)
    matrix = offdiag - identity * offdiag.sum(axis=1)[:, None]
    return jnp.asarray(matrix / level_count, dtype=jnp.float32)


def reference(velocity, test_fields, order_slots):
    phases = phase_table(order_slots, 0, NPHI, NPHI).astype(jnp.float32)
    live_map = live_mask(order_slots, jnp.arange(NTH, dtype=jnp.int32), M, NTH)
    vel_live = velocity * live_map.astype(jnp.bfloat16)
    tst_live = test_fields.reshape(NR, 6, 2, M, NTH) * live_map.astype(jnp.bfloat16)
    cycle_block = 128

    def one_block(first_cycle):
        vel_block = lax.dynamic_slice_in_dim(vel_live, first_cycle, cycle_block, 4).astype(jnp.float32)
        tst_block = lax.dynamic_slice_in_dim(tst_live, first_cycle, cycle_block, 4).astype(jnp.float32)
        live_block = lax.dynamic_slice_in_dim(live_map, first_cycle, cycle_block, 1).astype(jnp.float32)
        vel_cycle = jnp.einsum("lcksj,ksp->lcjp", vel_block, phases)
        tst_cycle = jnp.einsum("lcksj,ksp->lcjp", tst_block, phases).reshape(NR, 2, 3, cycle_block, NPHI)
        emf_cycle = jnp.cross(vel_cycle[:, None], tst_cycle, axis=2).astype(jnp.bfloat16)
        emf_cycle = emf_cycle.reshape(NR, 6, cycle_block, NPHI).astype(jnp.float32)
        spectrum = jnp.einsum("lgjp,ksp->lgksj", emf_cycle, phases)
        return (spectrum * (NPHI ** -0.5) * live_block).astype(jnp.bfloat16)

    starts = jnp.arange(NTH // cycle_block, dtype=jnp.int32) * cycle_block
    spectra = lax.map(one_block, starts)
    emf_out = jnp.moveaxis(spectra, 0, 4).reshape(NR, 2, 3, 2, M, NTH)
    deriv_mat = cheb_matrix(NR)
    emf_deriv = jnp.tensordot(deriv_mat, emf_out.astype(jnp.float32), axes=1, precision=lax.Precision.HIGHEST)
    return emf_out, emf_deriv.astype(jnp.bfloat16)
```

```python
import functools

import jax
import jax.numpy as jnp
import numpy as np
from jax import lax
from jax.experimental import pallas as pl
from jax.experimental.pallas import tpu as pltpu
from jax.sharding import PartitionSpec as P

MESH = pl.DeviceIdType.MESH
M = 1024
NTH = 1536
NPHI = 3072
HALF = NPHI // 2
NR = 4
NMA = 64
F32 = jnp.float32
BF16 = jnp.bfloat16
I32 = jnp.int32
PB = 256


def cheb_matrix(level_count):
    levels_at = np.arange(level_count)
    points = np.cos(np.pi * levels_at / (level_count - 1))
    weights = np.where((levels_at == 0) | (levels_at == level_count - 1), 2.0, 1.0) * np.where(
        levels_at % 2 == 0, 1.0, -1.0
    )
    identity = np.eye(level_count)
    spread = points[:, None] - points[None, :] + identity
    offdiag = weights[:, None] / weights[None, :] / spread * (1.0 - identity)
    matrix = offdiag - identity * offdiag.sum(axis=1)[:, None]
    return np.asarray(matrix / level_count, dtype=np.float32)


DERIV = cheb_matrix(NR)


def phase_tables():
    r = np.arange(M // 2)
    p = np.arange(HALF)
    tabs = []
    for m in (2 * r, M - 1 - 2 * r):
        q = (m[:, None] * p[None, :]) % NPHI
        ang = q.astype(np.float32) * np.float32(2.0 * np.pi / NPHI)
        tabs.append(np.concatenate([np.cos(ang), -np.sin(ang)], axis=0).astype(jnp.bfloat16))
    inv = np.stack(tabs)
    fwd = np.ascontiguousarray(np.swapaxes(inv, 1, 2))
    return fwd, inv


def expand_table():
    tab = np.zeros((3, 128, 256), np.float32)
    groups = []
    for f in range(2):
        for g, c in enumerate((1, 2, 0, 1)):
            groups.append((12 * (4 * f + g), c))
    b_first = 128 + 116
    for f in range(2):
        base = 3 + 3 * f
        for g, c in enumerate((2, 0, 1)):
            groups.append((128 + 12 * (4 * f + g), base + c))
        groups.append((b_first if f == 0 else 128 + 36, base + 1))
    for lane0, c in groups:
        for h in range(2):
            for v in range(6):
                lane = lane0 + h * 6 + v
                tab[0, c * 12 + h * 6 + v, lane] = 1
                tab[1, c * 12 + (1 - h) * 6 + v, lane] = 1
                tab[2, 108 + h * 9 + c, lane] = 1
    return np.concatenate(list(tab), axis=1).astype(jnp.bfloat16)


OUT_GROUPS = (0, 1, 2, 4, 5, 6)


def fold_table():
    tab = np.zeros((2, 128, 128), np.float32)
    for g, grp in enumerate(OUT_GROUPS):
        for h in range(2):
            for v in range(6):
                lane = grp * 12 + h * 6 + v
                tab[0, grp * 12 + (1 - h) * 6 + v, lane] = 1
                tab[1, lane, 96 + h * 6 + g] = 1
    return np.concatenate(list(tab), axis=0).astype(jnp.bfloat16)


def dot(a, b):
    return jnp.dot(a, b, preferred_element_type=F32)


def iota(shape, dim):
    return lax.broadcasted_iota(I32, shape, dim)


def onehot(cond):
    return jnp.where(cond, 1.0, 0.0).astype(BF16)


def cross(x):
    a, b = x[:, :128], x[:, 128:]
    return a * b - pltpu.roll(a, 116, 1) * pltpu.roll(b, 12, 1)


def kernel(
    vel_ref, tst_ref, own_ref, tgtc_ref, tgtr_ref, keyc_ref, keyr_ref, exp_ref, fold_ref, fwd_hbm, inv_hbm,
    emf_ref, der_ref,
    fwd_tab, inv_tab, packed, turned, sendbuf, recvbuf, perm, permt, rhs_e, rhs_o, summed, differ, pout,
    outbuf, backbuf, radbuf, dersend, derbuf, quse, qback, rows,
    tab_sem, f_send, f_recv, b_send, b_recv, y_send, y_recv, d_send, d_recv,
):
    me = lax.axis_index("ma")
    lev = lax.axis_index("rad")

    barrier = pltpu.get_barrier_semaphore()

    def greet(step, carry):
        pl.semaphore_signal(
            barrier, inc=1, device_id=(lev, lax.rem(me + step, NMA)), device_id_type=MESH
        )
        return carry

    lax.fori_loop(1, NMA, greet, 0)
    for step in range(1, NR):
        pl.semaphore_signal(barrier, inc=1, device_id=(lax.rem(lev + step, NR), me), device_id_type=MESH)

    tab_f = pltpu.make_async_copy(fwd_hbm, fwd_tab, tab_sem.at[0])
    tab_i = pltpu.make_async_copy(inv_hbm, inv_tab, tab_sem.at[1])
    tab_f.start()
    tab_i.start()

    quse[...] = onehot(tgtc_ref[0:192] == iota((192, 192), 1))
    qback[...] = onehot(tgtr_ref[:, 0:192] == iota((192, 192), 0))
    even = own_ref[...]
    odd = (M - 1) - even
    lane = iota((16, 128), 1)

    def masks(v):
        out = []
        for h in range(2):
            j = 128 * v + lane
            near = (j + 1) if h == 0 else (768 - j)
            out.append((even * NTH <= 2 * M * near, odd * NTH <= 2 * M * near))
        return out

    left = {}
    for w in range(3):
        halves = []
        for h in range(2):
            cols = slice(768 * h + 256 * w, 768 * h + 256 * w + 256)
            halves.append(
                (dot(quse[0:96, 0:96], vel_ref[:, cols]), dot(quse[...], tst_ref[:, cols]))
            )
        for vv in range(2):
            v = 2 * w + vv
            live = masks(v)
            for c in range(9):
                xe, xo = [], []
                for h in range(2):
                    src = halves[h][0] if c < 3 else halves[h][1]
                    row = 32 * (c if c < 3 else c - 3)
                    xe.append(src[row : row + 16, 128 * vv : 128 * vv + 128])
                    xo.append(src[row + 16 : row + 32, 128 * vv : 128 * vv + 128])
                for h in range(2):
                    spot = (c * 12 + h * 6 + v) * 16
                    packed[spot : spot + 16, :] = jnp.where(live[h][0], xe[h], xo[1 - h])
                    rest = jnp.where(live[h][1] & live[1 - h][0], xo[h], 0.0)
                    left[h, c] = rest if v == 0 else left[h, c] + rest
    for h in range(2):
        for c in range(9):
            spot = (108 + h * 9 + c) * 16
            packed[spot : spot + 16, :] = left[h, c]
    packed[126 * 16 : 128 * 16, :] = jnp.zeros((32, 128), F32)
    for row in range(16):
        turned[pl.ds(row, 128, stride=16), :] = packed[pl.ds(row, 128, stride=16), :].T
    sendbuf[...] = turned[...].astype(BF16).reshape(128, 16, 128)

    pl.semaphore_wait(barrier, NMA - 1 + NR - 1)

    def all_to_all(src, dst, ssem, rsem, u):
        def one(step, carry):
            to = lax.rem(me + step, NMA)
            pltpu.make_async_remote_copy(
                src_ref=src.at[u * NMA + to],
                dst_ref=dst.at[u * NMA + me],
                send_sem=ssem.at[u],
                recv_sem=rsem.at[u],
                device_id=(lev, to),
                device_id_type=MESH,
            ).start()
            return carry

        pltpu.make_async_copy(src.at[u * NMA + me], dst.at[u * NMA + me], rsem.at[u]).start()
        lax.fori_loop(1, NMA, one, 0)

    def wait_bytes(ref, sem):
        pltpu.make_async_copy(ref, ref, sem).wait()

    for u in range(2):
        all_to_all(sendbuf, recvbuf, f_send, f_recv, u)

    for b in range(4):
        blk = slice(256 * b, 256 * b + 256)
        perm[blk, :] = onehot(keyr_ref[...] == iota((256, 1024), 0) + 256 * b)
        permt[blk, :] = onehot(keyc_ref[blk] == iota((256, 1024), 1))

    tab_f.wait()
    tab_i.wait()

    def near_of(lane_id, u):
        l12 = jnp.where(lane_id >= 116, lane_id - 116, lax.rem(lane_id, 12))
        h = l12 >= 6
        v = jnp.where(h, l12 - 6, l12)
        j = 128 * v + 64 * u + me
        return jnp.where(h, 768 - j, j + 1)

    scale = NPHI ** (-0.5)

    for u in range(2):
        wait_bytes(recvbuf.at[pl.ds(u * NMA, NMA)], f_recv.at[u])
        got = recvbuf[u * NMA : (u + 1) * NMA].reshape(1024, 128)
        lane2 = lax.rem(iota((256, 256), 1), 128)
        near2 = near_of(lane2, u)
        for b in range(4):
            blk = slice(256 * b, 256 * b + 256)
            r = iota((256, 256), 0) + 256 * (b % 2)
            own_live = 3 * r <= 2 * near2
            far_live = 3 * r <= 2 * (769 - near2)
            odd_live = 3 * ((M - 1) - 2 * r) <= 4 * near2
            sorted_blk = dot(perm[blk, :], got).astype(BF16)
            wide = dot(sorted_blk, exp_ref[...])
            rhs_e[blk, :] = jnp.where(own_live, wide[:, 0:256], 0.0).astype(BF16)
            other = jnp.where(far_live, wide[:, 512:768], wide[:, 256:512])
            rhs_o[blk, :] = jnp.where(odd_live, other, 0.0).astype(BF16)

        def longitudes(i, carry):
            spot = pl.ds(pl.multiple_of(i * PB, PB), PB)
            ve = dot(fwd_tab[0, spot, :], rhs_e[...])
            vo = dot(fwd_tab[1, spot, :], rhs_o[...])
            first = cross(ve + vo)
            second = cross(ve - vo)
            summed[spot, :] = (first + second).astype(BF16)
            differ[spot, :] = (first - second).astype(BF16)
            return carry

        lax.fori_loop(0, HALF // PB, longitudes, 0)

        lane1 = iota((256, 128), 1)
        near1 = near_of(lane1, u)
        main = lane1 < 96
        for b in range(4):
            blk = slice(256 * b, 256 * b + 256)
            r = iota((256, 128), 0) + 256 * (b % 2)
            own_live = (3 * r <= 2 * near1) & main
            both_live = (3 * ((M - 1) - 2 * r) <= 4 * near1) & (3 * r <= 2 * (769 - near1)) & main
            se = dot(inv_tab[0, blk, :], summed[...]) * scale
            so = dot(inv_tab[1, blk, :], differ[...]) * scale
            so = so.astype(BF16)
            rest = jnp.where(both_live, so.astype(F32), 0.0).astype(BF16)
            moved = dot(so, fold_ref[0:128, :]) + dot(rest, fold_ref[128:256, :])
            pout[blk, :] = jnp.where(own_live, se, moved).astype(BF16)
        for b in range(4):
            blk = slice(256 * b, 256 * b + 256)
            outbuf[u * NMA + 16 * b : u * NMA + 16 * b + 16] = (
                dot(permt[blk, :], pout[...]).astype(BF16).reshape(16, 16, 128)
            )
        all_to_all(outbuf, backbuf, b_send, b_recv, u)

    def rad_send(u):
        for step in range(1, NR):
            to = lax.rem(lev + step, NR)
            pltpu.make_async_remote_copy(
                src_ref=backbuf.at[pl.ds(u * NMA + 16 * to, 16)],
                dst_ref=radbuf.at[u, lev],
                send_sem=y_send.at[u],
                recv_sem=y_recv.at[u],
                device_id=(to, me),
                device_id_type=MESH,
            ).start()
        pltpu.make_async_copy(
            backbuf.at[pl.ds(u * NMA + 16 * lev, 16)], radbuf.at[u, lev], y_recv.at[u]
        ).start()

    def rad_derive(u):
        wait_bytes(radbuf.at[u], y_recv.at[u])
        vals = [radbuf[u, k].astype(F32) for k in range(NR)]
        for i in range(NR):
            acc = vals[0] * float(DERIV[i, 0])
            for k in range(1, NR):
                acc = acc + vals[k] * float(DERIV[i, k])
            dersend[u, i] = acc.astype(BF16)
        for step in range(1, NR):
            to = lax.rem(lev + step, NR)
            pltpu.make_async_remote_copy(
                src_ref=dersend.at[u, to],
                dst_ref=derbuf.at[pl.ds(u * NMA + 16 * lev, 16)],
                send_sem=d_send.at[u],
                recv_sem=d_recv.at[u],
                device_id=(to, me),
                device_id_type=MESH,
            ).start()
        pltpu.make_async_copy(
            dersend.at[u, lev], derbuf.at[pl.ds(u * NMA + 16 * lev, 16)], d_recv.at[u]
        ).start()

    def unpack(buf, out_ref):
        turned[...] = buf[...].astype(F32).reshape(2048, 128)
        for row in range(16):
            packed[pl.ds(row, 128, stride=16), :] = turned[pl.ds(row, 128, stride=16), :].T
        for v in range(6):
            live = masks(v)
            for g, grp in enumerate(OUT_GROUPS):
                half = []
                for h in range(2):
                    spot = (grp * 12 + h * 6 + v) * 16
                    half.append(packed[spot : spot + 16, :])
                for h in range(2):
                    spot = (96 + h * 6 + g) * 16
                    rest = packed[spot : spot + 16, :]
                    cols = slice(768 * h + 128 * v, 768 * h + 128 * v + 128)
                    rows[32 * g : 32 * g + 16, cols] = jnp.where(live[h][0], half[h], 0.0).astype(BF16)
                    other = jnp.where(live[1 - h][0], rest, half[1 - h])
                    rows[32 * g + 16 : 32 * g + 32, cols] = jnp.where(live[h][1], other, 0.0).astype(BF16)
        for w in range(6):
            cols = slice(256 * w, 256 * w + 256)
            out_ref[:, cols] = dot(qback[...], rows[:, cols]).astype(BF16)

    wait_bytes(backbuf.at[pl.ds(0, NMA)], b_recv.at[0])
    rad_send(0)
    wait_bytes(backbuf.at[pl.ds(NMA, NMA)], b_recv.at[1])
    rad_send(1)
    rad_derive(0)
    unpack(backbuf, emf_ref)
    rad_derive(1)
    for u in range(2):
        wait_bytes(derbuf.at[pl.ds(u * NMA, NMA)], d_recv.at[u])
    unpack(derbuf, der_ref)

    for u in range(2):
        wait_bytes(sendbuf.at[pl.ds(0, NMA - 1)], f_send.at[u])
        wait_bytes(outbuf.at[pl.ds(0, NMA - 1)], b_send.at[u])
        wait_bytes(backbuf.at[pl.ds(0, 16 * (NR - 1))], y_send.at[u])
        wait_bytes(dersend.at[u, pl.ds(0, NR - 1)], d_send.at[u])


def per_device(velocity, test_fields, order_slots):
    me = lax.axis_index("ma")
    vel = velocity.reshape(3 * 2 * 16, NTH)
    tst = test_fields.reshape(6 * 2 * 16, NTH)
    firsts = order_slots.reshape(NMA, 8, 2)[:, :, 0]
    evens = jnp.where(firsts % 2 == 0, firsts, M - 1 - firsts)
    key = evens[:, None, :] // 2 + (512 * jnp.arange(2, dtype=I32))[None, :, None]
    key = key.reshape(1024)
    own_first = lax.dynamic_slice_in_dim(firsts, me, 1)[0]
    flag = own_first % 2
    own_even = jnp.where(flag == 0, own_first, M - 1 - own_first)
    own = jnp.broadcast_to(own_even[None, :], (2, 8)).reshape(16, 1)
    comp = jnp.arange(6, dtype=I32)[:, None, None, None]
    eo = jnp.arange(2, dtype=I32)[None, :, None, None]
    kk = jnp.arange(2, dtype=I32)[None, None, :, None]
    ii = jnp.arange(8, dtype=I32)[None, None, None, :]
    tgt = (32 * comp + 16 * kk + 2 * ii + jnp.bitwise_xor(eo, flag[None, None, None, :])).reshape(192)
    fwd, inv = phase_tables()
    vm = pl.BlockSpec(memory_space=pltpu.VMEM)
    hbm = pl.BlockSpec(memory_space=pl.ANY)
    dma = pltpu.SemaphoreType.DMA
    emf, der = pl.pallas_call(
        kernel,
        out_shape=[jax.ShapeDtypeStruct((192, NTH), BF16)] * 2,
        in_specs=[vm] * 9 + [hbm] * 2,
        out_specs=[vm] * 2,
        scratch_shapes=[
            pltpu.VMEM((2, HALF, 1024), BF16),
            pltpu.VMEM((2, 1024, HALF), BF16),
            pltpu.VMEM((2048, 128), F32),
            pltpu.VMEM((2048, 128), F32),
            pltpu.VMEM((128, 16, 128), BF16),
            pltpu.VMEM((128, 16, 128), BF16),
            pltpu.VMEM((1024, 1024), BF16),
            pltpu.VMEM((1024, 1024), BF16),
            pltpu.VMEM((1024, 256), BF16),
            pltpu.VMEM((1024, 256), BF16),
            pltpu.VMEM((HALF, 128), BF16),
            pltpu.VMEM((HALF, 128), BF16),
            pltpu.VMEM((1024, 128), BF16),
            pltpu.VMEM((128, 16, 128), BF16),
            pltpu.VMEM((128, 16, 128), BF16),
            pltpu.VMEM((2, NR, 16, 16, 128), BF16),
            pltpu.VMEM((2, NR, 16, 16, 128), BF16),
            pltpu.VMEM((128, 16, 128), BF16),
            pltpu.VMEM((192, 192), BF16),
            pltpu.VMEM((192, 192), BF16),
            pltpu.VMEM((192, NTH), BF16),
        ]
        + [dma((2,))] * 9,
        compiler_params=pltpu.CompilerParams(
            collective_id=0, has_side_effects=True, vmem_limit_bytes=48 << 20
        ),
    )(
        vel, tst, own, tgt.reshape(192, 1), tgt.reshape(1, 192), key.reshape(1024, 1), key.reshape(1, 1024),
        jnp.asarray(expand_table()), jnp.asarray(fold_table()), jnp.asarray(fwd), jnp.asarray(inv),
    )
    shape = (1, 2, 3, 2, 16, NTH)
    return emf.reshape(shape), der.reshape(shape)


def solution(mesh):
    return jax.shard_map(
        per_device,
        mesh=mesh,
        in_specs=(P("rad", None, None, "ma", None), P("rad", None, None, None, "ma", None), P()),
        out_specs=(P("rad", None, None, None, "ma", None), P("rad", None, None, None, "ma", None)),
        check_vma=False,
    )
```

```python
import functools

import jax
import jax.numpy as jnp
import numpy as np
from jax import lax
from jax.experimental import pallas as pl
from jax.experimental.pallas import tpu as pltpu
from jax.sharding import PartitionSpec as P

MESH = pl.DeviceIdType.MESH
M = 1024
NTH = 1536
NPHI = 3072
QUART = NPHI // 4
PAIRS = M // 2
NR = 4
NMA = 64
F32 = jnp.float32
BF16 = jnp.bfloat16
I32 = jnp.int32
PB = 256
EMF_HOME = (False, True)


def cheb_matrix(level_count):
    levels_at = np.arange(level_count)
    points = np.cos(np.pi * levels_at / (level_count - 1))
    weights = np.where((levels_at == 0) | (levels_at == level_count - 1), 2.0, 1.0) * np.where(
        levels_at % 2 == 0, 1.0, -1.0
    )
    identity = np.eye(level_count)
    spread = points[:, None] - points[None, :] + identity
    offdiag = weights[:, None] / weights[None, :] / spread * (1.0 - identity)
    matrix = offdiag - identity * offdiag.sum(axis=1)[:, None]
    return np.asarray(matrix / level_count, dtype=np.float32)


DERIV = cheb_matrix(NR)


def phase_tables():
    r = np.arange(M // 2)
    p = np.arange(QUART + 1)
    fwd = np.zeros((2, 2, QUART + 16, M // 2), np.float32)
    inv = np.zeros((2, 2, M // 2, QUART), np.float32)
    for par, m in enumerate((2 * r, M - 1 - 2 * r)):
        q = (p[:, None] * m[None, :]) % NPHI
        ang = q.astype(np.float32) * np.float32(2.0 * np.pi / NPHI)
        for k, tab in enumerate((np.cos(ang), -np.sin(ang))):
            fwd[par, k, : QUART + 1] = tab
            inv[par, k] = tab[:QUART].T
    inv[:, :, :, 0] *= 0.5
    sign = np.where(r % 2 == 0, 1.0, -1.0)
    fwd[:, :, QUART] = 0.0
    fwd[0, 0, QUART] = sign
    fwd[1, 1, QUART] = sign
    return fwd.astype(jnp.bfloat16), inv.astype(jnp.bfloat16)


def expand_table():
    tab = np.zeros((3, 128, 256), np.float32)
    groups = []
    for f in range(2):
        for g, c in enumerate((1, 2, 0, 1)):
            groups.append((12 * (4 * f + g), c))
    b_first = 128 + 116
    for f in range(2):
        base = 3 + 3 * f
        for g, c in enumerate((2, 0, 1)):
            groups.append((128 + 12 * (4 * f + g), base + c))
        groups.append((b_first if f == 0 else 128 + 36, base + 1))
    for lane0, c in groups:
        for h in range(2):
            for v in range(6):
                lane = lane0 + h * 6 + v
                tab[0, c * 12 + h * 6 + v, lane] = 1
                tab[1, c * 12 + (1 - h) * 6 + v, lane] = 1
                tab[2, 108 + h * 9 + c, lane] = 1
    return np.concatenate(list(tab), axis=1).astype(jnp.bfloat16)


OUT_GROUPS = (0, 1, 2, 4, 5, 6)


def fold_table():
    tab = np.zeros((2, 128, 128), np.float32)
    for g, grp in enumerate(OUT_GROUPS):
        for h in range(2):
            for v in range(6):
                lane = grp * 12 + h * 6 + v
                tab[0, grp * 12 + (1 - h) * 6 + v, lane] = 1
                tab[1, lane, 96 + h * 6 + g] = 1
    return np.concatenate(list(tab), axis=0).astype(jnp.bfloat16)


def dot(a, b):
    return jnp.dot(a, b, preferred_element_type=F32)


def iota(shape, dim):
    return lax.broadcasted_iota(I32, shape, dim)


def onehot(cond):
    return jnp.where(cond, 1.0, 0.0).astype(BF16)


def cross(x):
    a, b = x[:, :128], x[:, 128:]
    return a * b - pltpu.roll(a, 116, 1) * pltpu.roll(b, 12, 1)


def kernel(
    slot_smem, slot_ref, vel_hbm, tst_hbm, exp_hbm, fold_hbm, fwd_hbm, inv_hbm,
    emf_ref, der_ref,
    vel_ref, tst_ref, exp_ref, fold_ref, fwd_raw, inv_raw, fwd_tab, inv_tab, packed, turned, sendbuf, recvbuf,
    perm, permt, triple, sign, rhs, folded, outbuf, backbuf, radbuf, dersend, derbuf, quse, qback, rows,
    load_sem, f_send, f_recv, b_send, b_recv, y_send, y_recv, d_send, d_recv, own_send, e_send, ready,
):
    me = lax.axis_index("ma")
    lev = lax.axis_index("rad")

    barrier = pltpu.get_barrier_semaphore()

    def greet(step, carry):
        pl.semaphore_signal(
            barrier, inc=1, device_id=(lev, lax.rem(me + step, NMA)), device_id_type=MESH
        )
        return carry

    loads = [
        pltpu.make_async_copy(src, dst, load_sem.at[i])
        for i, (src, dst) in enumerate(
            (
                (vel_hbm, vel_ref), (tst_hbm, tst_ref), (fwd_hbm, fwd_raw), (inv_hbm, inv_raw),
                (exp_hbm, exp_ref), (fold_hbm, fold_ref),
            )
        )
    ]
    loads[0].start()
    loads[1].start()
    lax.fori_loop(1, NMA, greet, 0)
    for step in range(1, NR):
        pl.semaphore_signal(barrier, inc=1, device_id=(lax.rem(lev + step, NR), me), device_id_type=MESH)
    for load in loads[2:]:
        load.start()

    firsts = [slot_smem[me * 16 + 2 * i] for i in range(8)]

    def spread(pair, shape):
        out = jnp.full(shape, firsts[7], I32)
        for i in range(7):
            out = jnp.where(pair == i, firsts[i], out)
        return out

    def onehot_rows(dim):
        here = iota((192, 192), dim)
        first = spread(here & 7, (192, 192))
        slot = (here & ~31) + ((here & 8) << 1) + 2 * (here & 7) + (((here >> 4) ^ first) & 1)
        return onehot(slot == iota((192, 192), 1 - dim))

    quse[...] = onehot_rows(0)
    qback[...] = onehot_rows(1)
    lane = iota((16, 128), 1)
    first = spread(iota((16, 128), 0) & 7, (16, 128))
    even = jnp.where((first & 1) == 0, first, (M - 1) - first)
    odd = (M - 1) - even

    def masks(v):
        out = []
        for h in range(2):
            j = 128 * v + lane
            near = (j + 1) if h == 0 else (768 - j)
            out.append((even * NTH <= 2 * M * near, odd * NTH <= 2 * M * near))
        return out

    loads[0].wait()
    loads[1].wait()
    left = {}
    for w in range(3):
        halves = []
        for h in range(2):
            cols = slice(768 * h + 256 * w, 768 * h + 256 * w + 256)
            halves.append(
                (dot(quse[0:96, 0:96], vel_ref[:, cols]), dot(quse[...], tst_ref[:, cols]))
            )
        for vv in range(2):
            v = 2 * w + vv
            live = masks(v)
            for c in range(9):
                xe, xo = [], []
                for h in range(2):
                    src = halves[h][0] if c < 3 else halves[h][1]
                    row = 32 * (c if c < 3 else c - 3)
                    xe.append(src[row : row + 16, 128 * vv : 128 * vv + 128])
                    xo.append(src[row + 16 : row + 32, 128 * vv : 128 * vv + 128])
                for h in range(2):
                    spot = (c * 12 + h * 6 + v) * 16
                    packed[spot : spot + 16, :] = jnp.where(live[h][0], xe[h], xo[1 - h])
                    rest = jnp.where(live[h][1] & live[1 - h][0], xo[h], 0.0)
                    left[h, c] = rest if v == 0 else left[h, c] + rest
    for h in range(2):
        for c in range(9):
            spot = (108 + h * 9 + c) * 16
            packed[spot : spot + 16, :] = left[h, c]
    packed[126 * 16 : 128 * 16, :] = jnp.zeros((32, 128), F32)
    for row in range(16):
        turned[pl.ds(row, 128, stride=16), :] = packed[pl.ds(row, 128, stride=16), :].T
    sendbuf[...] = turned[...].astype(BF16).reshape(128, 16, 128)

    pl.semaphore_wait(barrier, NMA - 1 + NR - 1)
    for step in range(1, NR):
        pl.semaphore_signal(ready, inc=1, device_id=(lax.rem(lev + step, NR), me), device_id_type=MESH)

    def all_to_all(src, dst, ssem, rsem, u):
        def one(step, carry):
            to = lax.rem(me + step, NMA)
            pltpu.make_async_remote_copy(
                src_ref=src.at[u * NMA + to],
                dst_ref=dst.at[u * NMA + me],
                send_sem=ssem.at[u],
                recv_sem=rsem.at[u],
                device_id=(lev, to),
                device_id_type=MESH,
            ).start()
            return carry

        pltpu.make_async_copy(src.at[u * NMA + me], dst.at[u * NMA + me], rsem.at[u]).start()
        lax.fori_loop(1, NMA, one, 0)

    deriver = me // 16
    place = lax.rem(me, 16)

    def to_deriver(u):
        def one(step, carry):
            to = lax.rem(me + step, NMA)
            pltpu.make_async_remote_copy(
                src_ref=outbuf.at[u * NMA + to],
                dst_ref=radbuf.at[u, lev, place],
                send_sem=y_send.at[u],
                recv_sem=y_recv.at[u],
                device_id=(deriver, to),
                device_id_type=MESH,
            ).start()
            return carry

        lax.fori_loop(1, NMA, one, 0)

        @pl.when(deriver == lev)
        def _():
            pltpu.make_async_copy(outbuf.at[u * NMA + me], radbuf.at[u, lev, place], y_recv.at[u]).start()

        @pl.when(deriver != lev)
        def _():
            pltpu.make_async_remote_copy(
                src_ref=outbuf.at[u * NMA + me],
                dst_ref=radbuf.at[u, lev, place],
                send_sem=own_send.at[u],
                recv_sem=y_recv.at[u],
                device_id=(deriver, me),
                device_id_type=MESH,
            ).start()

    def wait_bytes(ref, sem):
        pltpu.make_async_copy(ref, ref, sem).wait()

    for u in range(2):
        all_to_all(sendbuf, recvbuf, f_send, f_recv, u)

    slots = slot_ref[...]
    rank = jnp.where((slots & 1) == 0, slots, (M - 1) - slots) >> 1
    high = (rank >> 4).astype(F32).astype(BF16)
    low = (rank & 15).astype(F32).astype(BF16)
    at_row, at_lane = iota((128, 128), 0), iota((128, 128), 1)
    parts = []
    for side in range(2):
        pick = onehot(at_row == 2 * (at_lane - 64 * side))
        parts.append(dot(high, pick) * 16.0 + dot(low, pick))
    keys = jnp.concatenate([parts[0][2 * b : 2 * b + 1] + parts[1][2 * b + 1 : 2 * b + 2] for b in range(4)] * 2, axis=0)
    keys_t = keys.T
    for b in range(4):
        blk = slice(128 * b, 128 * b + 128)
        perm[:, blk] = onehot(keys[b : b + 1, :] == iota((PAIRS, 128), 0).astype(F32))
        column = keys_t[:, b : b + 1]
        permt[blk, :] = onehot(column == iota((128, PAIRS), 1).astype(F32))
        wide = jnp.broadcast_to(column, (128, 128)).astype(I32)
        triple[blk, :] = 3 * wide
        sign[blk, :] = (1 - 2 * (wide & 1)).astype(F32)

    for load in loads[2:]:
        load.wait()

    def build(i, carry):
        for par in range(2):
            for k in range(2):
                spot = pl.ds(pl.multiple_of(i * 256, 256), 256)
                fwd_tab[par, k, spot, :] = dot(fwd_raw[par, k, spot, :], perm[...]).astype(BF16)
                inv_tab[par, k, :, spot] = dot(permt[...], inv_raw[par, k, :, spot]).astype(BF16)
        return carry

    lax.fori_loop(0, QUART // 256, build, 0)
    for par in range(2):
        for k in range(2):
            last = slice(QUART, QUART + 16)
            fwd_tab[par, k, last, :] = dot(fwd_raw[par, k, last, :], perm[...]).astype(BF16)

    def near_of(lane_id, u):
        l12 = jnp.where(lane_id >= 116, lane_id - 116, lax.rem(lane_id, 12))
        h = l12 >= 6
        v = jnp.where(h, l12 - 6, l12)
        j = 128 * v + 64 * u + me
        return jnp.where(h, 768 - j, j + 1)

    scale = NPHI ** (-0.5)

    for u in range(2):
        lane1 = iota((1, 128), 1)
        near = near_of(lane1, u)
        main = lane1 < 96
        own_top, far_top, odd_low = 2 * near, 1538 - 2 * near, 1535 - 2 * near
        wait_bytes(recvbuf.at[pl.ds(u * NMA, NMA)], f_recv.at[u])
        for b in range(4):
            blk = slice(128 * b, 128 * b + 128)
            got = recvbuf[u * NMA + 16 * b : u * NMA + 16 * b + 16].reshape(256, 128)
            wide = dot(got, exp_ref[...]).reshape(16, 2, 8, 768)
            tri = triple[blk, :]
            own_live = tri <= own_top
            far_live = tri <= far_top
            odd_live = tri >= odd_low
            for k in range(2):
                part = wide[:, k].reshape(128, 768)
                for t in range(2):
                    cols = slice(128 * t, 128 * t + 128)
                    same, swap, rest = (part[:, 256 * i + 128 * t : 256 * i + 128 * t + 128] for i in range(3))
                    rhs[0, k, blk, cols] = jnp.where(own_live, same, 0.0).astype(BF16)
                    other = jnp.where(far_live, rest, swap)
                    rhs[1, k, blk, cols] = jnp.where(odd_live, other, 0.0).astype(BF16)

        def longitudes(i, carry):
            spot = pl.ds(pl.multiple_of(i * PB, PB), PB)
            ce, se, co, so = (
                dot(fwd_tab[par, k, spot, :], rhs[par, k]) for par in range(2) for k in range(2)
            )
            ve, vo = ce + se, co + so
            me_, mo = ce - se, so - co
            e1, e2 = cross(ve + vo), cross(ve - vo)
            e3, e4 = cross(me_ + mo), cross(me_ - mo)
            us, ws, um, wm = e1 + e2, e1 - e2, e3 + e4, e3 - e4
            folded[0, 0, spot, :] = (us + um).astype(BF16)
            folded[0, 1, spot, :] = (us - um).astype(BF16)
            folded[1, 0, spot, :] = (ws - wm).astype(BF16)
            folded[1, 1, spot, :] = (ws + wm).astype(BF16)
            return carry

        lax.fori_loop(0, QUART // PB, longitudes, 0, unroll=True)
        last = slice(QUART, QUART + 16)
        ve, vo = (
            dot(fwd_tab[par, 0, last, :], rhs[par, 0]) + dot(fwd_tab[par, 1, last, :], rhs[par, 1])
            for par in range(2)
        )
        e1, e2 = cross(ve + vo), cross(ve - vo)
        quarter = ((e1 + e2)[0:1], (e1 - e2)[0:1])

        for b in range(2):
            blk = slice(256 * b, 256 * b + 256)
            tri = triple[blk, :]
            own_live = (tri <= own_top) & main
            both_live = (tri >= odd_low) & (tri <= far_top) & main
            out = []
            for k in range(2):
                se = dot(inv_tab[0, k, blk, :], folded[0, k])
                so = dot(inv_tab[1, k, blk, :], folded[1, k])
                if k == 0:
                    se = se + sign[blk, :] * quarter[0]
                else:
                    so = so + sign[blk, :] * quarter[1]
                so = so * scale
                rest = jnp.where(both_live, so, 0.0)
                moved = dot(jnp.concatenate([so, rest], axis=1).astype(BF16), fold_ref[...])
                out.append(jnp.where(own_live, se * scale, moved).reshape(32, 1, 8, 128))
            outbuf[u * NMA + 32 * b : u * NMA + 32 * b + 32] = (
                jnp.concatenate(out, axis=1).reshape(32, 16, 128).astype(BF16)
            )
        if u == 0:
            pl.semaphore_wait(ready, NR - 1)
        to_deriver(u)
        if EMF_HOME[u]:
            all_to_all(outbuf, backbuf, b_send, b_recv, u)

    def rad_derive(u):
        wait_bytes(radbuf.at[u], y_recv.at[u])
        vals = [radbuf[u, k].astype(F32) for k in range(NR)]
        for i in range(NR):
            acc = vals[0] * float(DERIV[i, 0])
            for k in range(1, NR):
                acc = acc + vals[k] * float(DERIV[i, k])
            dersend[u, i] = acc.astype(BF16)
        for step in range(1, NR):
            to = lax.rem(lev + step, NR)
            pltpu.make_async_remote_copy(
                src_ref=dersend.at[u, to],
                dst_ref=derbuf.at[pl.ds(u * NMA + 16 * lev, 16)],
                send_sem=d_send.at[u],
                recv_sem=d_recv.at[u],
                device_id=(to, me),
                device_id_type=MESH,
            ).start()
        pltpu.make_async_copy(
            dersend.at[u, lev], derbuf.at[pl.ds(u * NMA + 16 * lev, 16)], d_recv.at[u]
        ).start()
        if not EMF_HOME[u]:
            for step in range(1, NR):
                to = lax.rem(lev + step, NR)
                pltpu.make_async_remote_copy(
                    src_ref=radbuf.at[u, to],
                    dst_ref=backbuf.at[pl.ds(u * NMA + 16 * lev, 16)],
                    send_sem=e_send.at[u],
                    recv_sem=b_recv.at[u],
                    device_id=(to, me),
                    device_id_type=MESH,
                ).start()
            pltpu.make_async_copy(
                radbuf.at[u, lev], backbuf.at[pl.ds(u * NMA + 16 * lev, 16)], b_recv.at[u]
            ).start()

    def unpack(buf, out_ref):
        turned[...] = buf[...].astype(F32).reshape(2048, 128)
        for row in range(16):
            packed[pl.ds(row, 128, stride=16), :] = turned[pl.ds(row, 128, stride=16), :].T
        for v in range(6):
            live = masks(v)
            for g, grp in enumerate(OUT_GROUPS):
                half = []
                for h in range(2):
                    spot = (grp * 12 + h * 6 + v) * 16
                    half.append(packed[spot : spot + 16, :])
                for h in range(2):
                    spot = (96 + h * 6 + g) * 16
                    rest = packed[spot : spot + 16, :]
                    cols = slice(768 * h + 128 * v, 768 * h + 128 * v + 128)
                    rows[32 * g : 32 * g + 16, cols] = jnp.where(live[h][0], half[h], 0.0).astype(BF16)
                    other = jnp.where(live[1 - h][0], rest, half[1 - h])
                    rows[32 * g + 16 : 32 * g + 32, cols] = jnp.where(live[h][1], other, 0.0).astype(BF16)
        for w in range(6):
            cols = slice(256 * w, 256 * w + 256)
            out_ref[:, cols] = dot(qback[...], rows[:, cols]).astype(BF16)

    for u in range(2):
        rad_derive(u)
    for u in range(2):
        wait_bytes(backbuf.at[pl.ds(u * NMA, NMA)], b_recv.at[u])
    unpack(backbuf, emf_ref)
    for u in range(2):
        wait_bytes(derbuf.at[pl.ds(u * NMA, NMA)], d_recv.at[u])
    unpack(derbuf, der_ref)

    for u in range(2):
        wait_bytes(sendbuf.at[pl.ds(0, NMA - 1)], f_send.at[u])
        wait_bytes(outbuf.at[pl.ds(0, NMA - 1)], y_send.at[u])

        @pl.when(deriver != lev)
        def _():
            wait_bytes(outbuf.at[0], own_send.at[u])

        wait_bytes(dersend.at[u, pl.ds(0, NR - 1)], d_send.at[u])
        if EMF_HOME[u]:
            wait_bytes(outbuf.at[pl.ds(0, NMA - 1)], b_send.at[u])
        else:
            wait_bytes(radbuf.at[u, pl.ds(0, NR - 1)], e_send.at[u])


def per_device(velocity, test_fields, order_slots):
    vel = velocity.reshape(3 * 2 * 16, NTH)
    tst = test_fields.reshape(6 * 2 * 16, NTH)
    fwd, inv = phase_tables()
    vm = pl.BlockSpec(memory_space=pltpu.VMEM)
    sm = pl.BlockSpec(memory_space=pltpu.SMEM)
    hbm = pl.BlockSpec(memory_space=pl.ANY)
    dma = pltpu.SemaphoreType.DMA

    def vmem(*shape, dtype=BF16):
        return pltpu.VMEM(shape, dtype)

    emf, der = pl.pallas_call(
        kernel,
        out_shape=[jax.ShapeDtypeStruct((192, NTH), BF16)] * 2,
        in_specs=[sm, vm] + [hbm] * 6,
        out_specs=[vm] * 2,
        scratch_shapes=[
            vmem(96, NTH),
            vmem(192, NTH),
            vmem(128, 768),
            vmem(256, 128),
            vmem(2, 2, QUART + 16, PAIRS),
            vmem(2, 2, PAIRS, QUART),
            vmem(2, 2, QUART + 16, PAIRS),
            vmem(2, 2, PAIRS, QUART),
            vmem(2048, 128, dtype=F32),
            vmem(2048, 128, dtype=F32),
            vmem(128, 16, 128),
            vmem(128, 16, 128),
            vmem(PAIRS, PAIRS),
            vmem(PAIRS, PAIRS),
            vmem(PAIRS, 128, dtype=I32),
            vmem(PAIRS, 128, dtype=F32),
            vmem(2, 2, PAIRS, 256),
            vmem(2, 2, QUART, 128),
            vmem(128, 16, 128),
            vmem(128, 16, 128),
            vmem(2, NR, 16, 16, 128),
            vmem(2, NR, 16, 16, 128),
            vmem(128, 16, 128),
            vmem(192, 192),
            vmem(192, 192),
            vmem(192, NTH),
            dma((6,)),
        ]
        + [dma((2,))] * 10
        + [pltpu.SemaphoreType.REGULAR],
        compiler_params=pltpu.CompilerParams(
            collective_id=0, has_side_effects=True, vmem_limit_bytes=60 << 20
        ),
    )(
        order_slots, order_slots.reshape(8, 128), vel, tst,
        jnp.asarray(expand_table()), jnp.asarray(fold_table()), jnp.asarray(fwd), jnp.asarray(inv),
    )
    shape = (1, 2, 3, 2, 16, NTH)
    return emf.reshape(shape), der.reshape(shape)


def solution(mesh):
    return jax.shard_map(
        per_device,
        mesh=mesh,
        in_specs=(P("rad", None, None, "ma", None), P("rad", None, None, None, "ma", None), P()),
        out_specs=(P("rad", None, None, None, "ma", None), P("rad", None, None, None, "ma", None)),
        check_vma=False,
    )
```

```python
import functools

import jax
import jax.numpy as jnp
import numpy as np
from jax import lax
from jax.experimental import pallas as pl
from jax.experimental.pallas import tpu as pltpu
from jax.sharding import PartitionSpec as P

MESH = pl.DeviceIdType.MESH
M = 1024
NTH = 1536
NPHI = 3072
QUART = NPHI // 4
PAIRS = M // 2
NR = 4
NMA = 64
F32 = jnp.float32
BF16 = jnp.bfloat16
I32 = jnp.int32
PB = 256
EMF_HOME = (False, True)


def cheb_matrix(level_count):
    levels_at = np.arange(level_count)
    points = np.cos(np.pi * levels_at / (level_count - 1))
    weights = np.where((levels_at == 0) | (levels_at == level_count - 1), 2.0, 1.0) * np.where(
        levels_at % 2 == 0, 1.0, -1.0
    )
    identity = np.eye(level_count)
    spread = points[:, None] - points[None, :] + identity
    offdiag = weights[:, None] / weights[None, :] / spread * (1.0 - identity)
    matrix = offdiag - identity * offdiag.sum(axis=1)[:, None]
    return np.asarray(matrix / level_count, dtype=np.float32)


DERIV = cheb_matrix(NR)


def phase_tables():
    r = np.arange(M // 2)
    p = np.arange(QUART + 1)
    fwd = np.zeros((2, 2, QUART + 16, M // 2), np.float32)
    inv = np.zeros((2, 2, M // 2, QUART), np.float32)
    for par, m in enumerate((2 * r, M - 1 - 2 * r)):
        q = (p[:, None] * m[None, :]) % NPHI
        ang = q.astype(np.float32) * np.float32(2.0 * np.pi / NPHI)
        for k, tab in enumerate((np.cos(ang), -np.sin(ang))):
            fwd[par, k, : QUART + 1] = tab
            inv[par, k] = tab[:QUART].T
    inv[:, :, :, 0] *= 0.5
    sign = np.where(r % 2 == 0, 1.0, -1.0)
    fwd[:, :, QUART] = 0.0
    fwd[0, 0, QUART] = sign
    fwd[1, 1, QUART] = sign
    return fwd.astype(jnp.bfloat16), inv.astype(jnp.bfloat16)


def expand_table():
    tab = np.zeros((3, 128, 256), np.float32)
    groups = []
    for f in range(2):
        for g, c in enumerate((1, 2, 0, 1)):
            groups.append((12 * (4 * f + g), c))
    b_first = 128 + 116
    for f in range(2):
        base = 3 + 3 * f
        for g, c in enumerate((2, 0, 1)):
            groups.append((128 + 12 * (4 * f + g), base + c))
        groups.append((b_first if f == 0 else 128 + 36, base + 1))
    for lane0, c in groups:
        for h in range(2):
            for v in range(6):
                lane = lane0 + h * 6 + v
                tab[0, c * 12 + h * 6 + v, lane] = 1
                tab[1, c * 12 + (1 - h) * 6 + v, lane] = 1
                tab[2, 108 + h * 9 + c, lane] = 1
    return np.concatenate(list(tab), axis=1).astype(jnp.bfloat16)


OUT_GROUPS = (0, 1, 2, 4, 5, 6)


def fold_table():
    tab = np.zeros((2, 128, 128), np.float32)
    for g, grp in enumerate(OUT_GROUPS):
        for h in range(2):
            for v in range(6):
                lane = grp * 12 + h * 6 + v
                tab[0, grp * 12 + (1 - h) * 6 + v, lane] = 1
                tab[1, lane, 96 + h * 6 + g] = 1
    return np.concatenate(list(tab), axis=0).astype(jnp.bfloat16)


def dot(a, b):
    return jnp.dot(a, b, preferred_element_type=F32)


def iota(shape, dim):
    return lax.broadcasted_iota(I32, shape, dim)


def onehot(cond):
    return jnp.where(cond, 1.0, 0.0).astype(BF16)


def cross(x):
    a, b = x[:, :128], x[:, 128:]
    return a * b - pltpu.roll(a, 116, 1) * pltpu.roll(b, 12, 1)


def kernel(
    slot_smem, slot_ref, vel_hbm, tst_hbm, exp_hbm, fold_hbm, fwd_hbm, inv_hbm,
    emf_ref, der_ref,
    vel_ref, tst_ref, exp_ref, fold_ref, fwd_raw, inv_raw, fwd_tab, inv_tab, packed, turned, sendbuf, recvbuf,
    perm, permt, triple, sign, rhs, folded, outbuf, backbuf, radbuf, dersend, derbuf, quse, qback, rows,
    load_sem, f_send, f_recv, b_send, b_recv, y_send, y_recv, d_send, d_recv, own_send, e_send, ready,
):
    me = lax.axis_index("ma")
    lev = lax.axis_index("rad")

    barrier = pltpu.get_barrier_semaphore()

    def greet(step, carry):
        pl.semaphore_signal(
            barrier, inc=1, device_id=(lev, lax.rem(me + step, NMA)), device_id_type=MESH
        )
        return carry

    loads = [
        pltpu.make_async_copy(src, dst, load_sem.at[i])
        for i, (src, dst) in enumerate(
            (
                (vel_hbm, vel_ref), (tst_hbm, tst_ref), (fwd_hbm, fwd_raw), (inv_hbm, inv_raw),
                (exp_hbm, exp_ref), (fold_hbm, fold_ref),
            )
        )
    ]
    loads[0].start()
    loads[1].start()
    lax.fori_loop(1, NMA, greet, 0)
    for step in range(1, NR):
        pl.semaphore_signal(barrier, inc=1, device_id=(lax.rem(lev + step, NR), me), device_id_type=MESH)
    for load in loads[2:]:
        load.start()

    firsts = [slot_smem[me * 16 + 2 * i] for i in range(8)]

    def spread(pair, shape):
        out = jnp.full(shape, firsts[7], I32)
        for i in range(7):
            out = jnp.where(pair == i, firsts[i], out)
        return out

    def onehot_rows(dim):
        here = iota((192, 192), dim)
        first = spread(here & 7, (192, 192))
        slot = (here & ~31) + ((here & 8) << 1) + 2 * (here & 7) + (((here >> 4) ^ first) & 1)
        return onehot(slot == iota((192, 192), 1 - dim))

    quse[...] = onehot_rows(0)
    qback[...] = onehot_rows(1)
    lane = iota((16, 128), 1)
    first = spread(iota((16, 128), 0) & 7, (16, 128))
    even = jnp.where((first & 1) == 0, first, (M - 1) - first)
    odd = (M - 1) - even

    def masks(v):
        out = []
        for h in range(2):
            j = 128 * v + lane
            near = (j + 1) if h == 0 else (768 - j)
            out.append((even * NTH <= 2 * M * near, odd * NTH <= 2 * M * near))
        return out

    loads[0].wait()
    loads[1].wait()
    left = {}
    for w in range(3):
        halves = []
        for h in range(2):
            cols = slice(768 * h + 256 * w, 768 * h + 256 * w + 256)
            halves.append(
                (dot(quse[0:96, 0:96], vel_ref[:, cols]), dot(quse[...], tst_ref[:, cols]))
            )
        for vv in range(2):
            v = 2 * w + vv
            live = masks(v)
            for c in range(9):
                xe, xo = [], []
                for h in range(2):
                    src = halves[h][0] if c < 3 else halves[h][1]
                    row = 32 * (c if c < 3 else c - 3)
                    xe.append(src[row : row + 16, 128 * vv : 128 * vv + 128])
                    xo.append(src[row + 16 : row + 32, 128 * vv : 128 * vv + 128])
                for h in range(2):
                    spot = (c * 12 + h * 6 + v) * 16
                    packed[spot : spot + 16, :] = jnp.where(live[h][0], xe[h], xo[1 - h])
                    rest = jnp.where(live[h][1] & live[1 - h][0], xo[h], 0.0)
                    left[h, c] = rest if v == 0 else left[h, c] + rest
    for h in range(2):
        for c in range(9):
            spot = (108 + h * 9 + c) * 16
            packed[spot : spot + 16, :] = left[h, c]
    packed[126 * 16 : 128 * 16, :] = jnp.zeros((32, 128), F32)
    for row in range(16):
        turned[pl.ds(row, 128, stride=16), :] = packed[pl.ds(row, 128, stride=16), :].T
    sendbuf[...] = turned[...].astype(BF16).reshape(128, 16, 128)

    pl.semaphore_wait(barrier, NMA - 1 + NR - 1)
    for step in range(1, NR):
        pl.semaphore_signal(ready, inc=1, device_id=(lax.rem(lev + step, NR), me), device_id_type=MESH)

    def all_to_all(src, dst, ssem, rsem, u):
        def one(step, carry):
            to = lax.rem(me + step, NMA)
            pltpu.make_async_remote_copy(
                src_ref=src.at[u * NMA + to],
                dst_ref=dst.at[u * NMA + me],
                send_sem=ssem.at[u],
                recv_sem=rsem.at[u],
                device_id=(lev, to),
                device_id_type=MESH,
            ).start()
            return carry

        pltpu.make_async_copy(src.at[u * NMA + me], dst.at[u * NMA + me], rsem.at[u]).start()
        lax.fori_loop(1, NMA, one, 0)

    deriver = me // 16
    place = lax.rem(me, 16)

    def to_deriver(u):
        def one(step, carry):
            to = lax.rem(me + step, NMA)
            pltpu.make_async_remote_copy(
                src_ref=outbuf.at[u * NMA + to],
                dst_ref=radbuf.at[u, lev, place],
                send_sem=y_send.at[u],
                recv_sem=y_recv.at[u],
                device_id=(deriver, to),
                device_id_type=MESH,
            ).start()
            return carry

        lax.fori_loop(1, NMA, one, 0)

        @pl.when(deriver == lev)
        def _():
            pltpu.make_async_copy(outbuf.at[u * NMA + me], radbuf.at[u, lev, place], y_recv.at[u]).start()

        @pl.when(deriver != lev)
        def _():
            pltpu.make_async_remote_copy(
                src_ref=outbuf.at[u * NMA + me],
                dst_ref=radbuf.at[u, lev, place],
                send_sem=own_send.at[u],
                recv_sem=y_recv.at[u],
                device_id=(deriver, me),
                device_id_type=MESH,
            ).start()

    def wait_bytes(ref, sem):
        pltpu.make_async_copy(ref, ref, sem).wait()

    for u in range(2):
        all_to_all(sendbuf, recvbuf, f_send, f_recv, u)

    slots = slot_ref[...]
    rank = jnp.where((slots & 1) == 0, slots, (M - 1) - slots) >> 1
    high = (rank >> 4).astype(F32).astype(BF16)
    low = (rank & 15).astype(F32).astype(BF16)
    at_row, at_lane = iota((128, 128), 0), iota((128, 128), 1)
    parts = []
    for side in range(2):
        pick = onehot(at_row == 2 * (at_lane - 64 * side))
        parts.append(dot(high, pick) * 16.0 + dot(low, pick))
    keys = jnp.concatenate([parts[0][2 * b : 2 * b + 1] + parts[1][2 * b + 1 : 2 * b + 2] for b in range(4)] * 2, axis=0)
    keys_t = keys.T
    for b in range(4):
        blk = slice(128 * b, 128 * b + 128)
        perm[:, blk] = onehot(keys[b : b + 1, :] == iota((PAIRS, 128), 0).astype(F32))
        column = keys_t[:, b : b + 1]
        permt[blk, :] = onehot(column == iota((128, PAIRS), 1).astype(F32))
        wide = jnp.broadcast_to(column, (128, 128)).astype(I32)
        triple[blk, :] = 3 * wide
        sign[blk, :] = (1 - 2 * (wide & 1)).astype(F32)

    for load in loads[2:]:
        load.wait()

    def build(i, carry):
        for par in range(2):
            for k in range(2):
                spot = pl.ds(pl.multiple_of(i * 256, 256), 256)
                fwd_tab[par, k, spot, :] = dot(fwd_raw[par, k, spot, :], perm[...]).astype(BF16)
                inv_tab[par, k, :, spot] = dot(permt[...], inv_raw[par, k, :, spot]).astype(BF16)
        return carry

    lax.fori_loop(0, QUART // 256, build, 0)
    for par in range(2):
        for k in range(2):
            last = slice(QUART, QUART + 16)
            fwd_tab[par, k, last, :] = dot(fwd_raw[par, k, last, :], perm[...]).astype(BF16)

    def near_of(lane_id, u):
        l12 = jnp.where(lane_id >= 116, lane_id - 116, lax.rem(lane_id, 12))
        h = l12 >= 6
        v = jnp.where(h, l12 - 6, l12)
        j = 128 * v + 64 * u + me
        return jnp.where(h, 768 - j, j + 1)

    scale = NPHI ** (-0.5)

    for u in range(2):
        lane1 = iota((1, 128), 1)
        near = near_of(lane1, u)
        main = lane1 < 96
        own_top, far_top, odd_low = 2 * near, 1538 - 2 * near, 1535 - 2 * near
        wait_bytes(recvbuf.at[pl.ds(u * NMA, NMA)], f_recv.at[u])
        for b in range(4):
            blk = slice(128 * b, 128 * b + 128)
            got = recvbuf[u * NMA + 16 * b : u * NMA + 16 * b + 16].reshape(256, 128)
            wide = dot(got, exp_ref[...]).reshape(16, 2, 8, 768)
            tri = triple[blk, :]
            own_live = tri <= own_top
            far_live = tri <= far_top
            odd_live = tri >= odd_low
            for k in range(2):
                part = wide[:, k].reshape(128, 768)
                for t in range(2):
                    cols = slice(128 * t, 128 * t + 128)
                    same, swap, rest = (part[:, 256 * i + 128 * t : 256 * i + 128 * t + 128] for i in range(3))
                    rhs[0, k, blk, cols] = jnp.where(own_live, same, 0.0).astype(BF16)
                    other = jnp.where(far_live, rest, swap)
                    rhs[1, k, blk, cols] = jnp.where(odd_live, other, 0.0).astype(BF16)

        def longitudes(i, carry):
            spot = pl.ds(pl.multiple_of(i * PB, PB), PB)
            ce, se, co, so = (
                dot(fwd_tab[par, k, spot, :], rhs[par, k]) for par in range(2) for k in range(2)
            )
            ve, vo = ce + se, co + so
            me_, mo = ce - se, so - co
            e1, e2 = cross(ve + vo), cross(ve - vo)
            e3, e4 = cross(me_ + mo), cross(me_ - mo)
            us, ws, um, wm = e1 + e2, e1 - e2, e3 + e4, e3 - e4
            folded[0, 0, spot, :] = (us + um).astype(BF16)
            folded[0, 1, spot, :] = (us - um).astype(BF16)
            folded[1, 0, spot, :] = (ws - wm).astype(BF16)
            folded[1, 1, spot, :] = (ws + wm).astype(BF16)
            return carry

        lax.fori_loop(0, QUART // PB, longitudes, 0, unroll=True)
        last = slice(QUART, QUART + 16)
        ve, vo = (
            dot(fwd_tab[par, 0, last, :], rhs[par, 0]) + dot(fwd_tab[par, 1, last, :], rhs[par, 1])
            for par in range(2)
        )
        e1, e2 = cross(ve + vo), cross(ve - vo)
        quarter = ((e1 + e2)[0:1], (e1 - e2)[0:1])

        for b in range(2):
            blk = slice(256 * b, 256 * b + 256)
            tri = triple[blk, :]
            own_live = (tri <= own_top) & main
            both_live = (tri >= odd_low) & (tri <= far_top) & main
            out = []
            for k in range(2):
                se = dot(inv_tab[0, k, blk, :], folded[0, k])
                so = dot(inv_tab[1, k, blk, :], folded[1, k])
                if k == 0:
                    se = se + sign[blk, :] * quarter[0]
                else:
                    so = so + sign[blk, :] * quarter[1]
                so = so * scale
                rest = jnp.where(both_live, so, 0.0)
                moved = dot(jnp.concatenate([so, rest], axis=1).astype(BF16), fold_ref[...])
                out.append(jnp.where(own_live, se * scale, moved).reshape(32, 1, 8, 128))
            outbuf[u * NMA + 32 * b : u * NMA + 32 * b + 32] = (
                jnp.concatenate(out, axis=1).reshape(32, 16, 128).astype(BF16)
            )
        if u == 0:
            pl.semaphore_wait(ready, NR - 1)
        to_deriver(u)
        if EMF_HOME[u]:
            all_to_all(outbuf, backbuf, b_send, b_recv, u)

    def rad_derive(u):
        wait_bytes(radbuf.at[u], y_recv.at[u])
        vals = [radbuf[u, k].astype(F32) for k in range(NR)]
        for i in range(NR):
            acc = vals[0] * float(DERIV[i, 0])
            for k in range(1, NR):
                acc = acc + vals[k] * float(DERIV[i, k])
            dersend[u, i] = acc.astype(BF16)
        for step in range(1, NR):
            to = lax.rem(lev + step, NR)
            pltpu.make_async_remote_copy(
                src_ref=dersend.at[u, to],
                dst_ref=derbuf.at[pl.ds(u * NMA + 16 * lev, 16)],
                send_sem=d_send.at[u],
                recv_sem=d_recv.at[u],
                device_id=(to, me),
                device_id_type=MESH,
            ).start()
        pltpu.make_async_copy(
            dersend.at[u, lev], derbuf.at[pl.ds(u * NMA + 16 * lev, 16)], d_recv.at[u]
        ).start()
        if not EMF_HOME[u]:
            for step in range(1, NR):
                to = lax.rem(lev + step, NR)
                pltpu.make_async_remote_copy(
                    src_ref=radbuf.at[u, to],
                    dst_ref=backbuf.at[pl.ds(u * NMA + 16 * lev, 16)],
                    send_sem=e_send.at[u],
                    recv_sem=b_recv.at[u],
                    device_id=(to, me),
                    device_id_type=MESH,
                ).start()
            pltpu.make_async_copy(
                radbuf.at[u, lev], backbuf.at[pl.ds(u * NMA + 16 * lev, 16)], b_recv.at[u]
            ).start()

    def unpack(buf, out_ref):
        turned[...] = buf[...].astype(F32).reshape(2048, 128)
        for row in range(16):
            packed[pl.ds(row, 128, stride=16), :] = turned[pl.ds(row, 128, stride=16), :].T
        for v in range(6):
            live = masks(v)
            for g, grp in enumerate(OUT_GROUPS):
                half = []
                for h in range(2):
                    spot = (grp * 12 + h * 6 + v) * 16
                    half.append(packed[spot : spot + 16, :])
                for h in range(2):
                    spot = (96 + h * 6 + g) * 16
                    rest = packed[spot : spot + 16, :]
                    cols = slice(768 * h + 128 * v, 768 * h + 128 * v + 128)
                    rows[32 * g : 32 * g + 16, cols] = jnp.where(live[h][0], half[h], 0.0).astype(BF16)
                    other = jnp.where(live[1 - h][0], rest, half[1 - h])
                    rows[32 * g + 16 : 32 * g + 32, cols] = jnp.where(live[h][1], other, 0.0).astype(BF16)
        for w in range(6):
            cols = slice(256 * w, 256 * w + 256)
            out_ref[:, cols] = dot(qback[...], rows[:, cols]).astype(BF16)

    for u in range(2):
        rad_derive(u)
    for u in range(2):
        wait_bytes(backbuf.at[pl.ds(u * NMA, NMA)], b_recv.at[u])
    unpack(backbuf, emf_ref)
    for u in range(2):
        wait_bytes(derbuf.at[pl.ds(u * NMA, NMA)], d_recv.at[u])
    unpack(derbuf, der_ref)

    for u in range(2):
        wait_bytes(sendbuf.at[pl.ds(0, NMA - 1)], f_send.at[u])
        wait_bytes(outbuf.at[pl.ds(0, NMA - 1)], y_send.at[u])

        @pl.when(deriver != lev)
        def _():
            wait_bytes(outbuf.at[0], own_send.at[u])

        wait_bytes(dersend.at[u, pl.ds(0, NR - 1)], d_send.at[u])
        if EMF_HOME[u]:
            wait_bytes(outbuf.at[pl.ds(0, NMA - 1)], b_send.at[u])
        else:
            wait_bytes(radbuf.at[u, pl.ds(0, NR - 1)], e_send.at[u])


def settle(emf_in, der_in, emf_out, der_out, sem):
    copies = []
    for i, (a, b) in enumerate(((emf_in, emf_out), (der_in, der_out))):
        for part in range(6):
            blk = pl.ds(part * (192 // 6), 192 // 6)
            copies.append(pltpu.make_async_copy(a.at[blk], b.at[blk], sem.at[i, part]))
    for copy in copies:
        copy.start()
    for copy in copies:
        copy.wait()


def per_device(velocity, test_fields, order_slots):
    vel = velocity.reshape(3 * 2 * 16, NTH)
    tst = test_fields.reshape(6 * 2 * 16, NTH)
    fwd, inv = phase_tables()
    vm = pl.BlockSpec(memory_space=pltpu.VMEM)
    sm = pl.BlockSpec(memory_space=pltpu.SMEM)
    hbm = pl.BlockSpec(memory_space=pl.ANY)
    dma = pltpu.SemaphoreType.DMA

    def vmem(*shape, dtype=BF16):
        return pltpu.VMEM(shape, dtype)

    emf, der = pl.pallas_call(
        kernel,
        out_shape=[jax.ShapeDtypeStruct((192, NTH), BF16)] * 2,
        in_specs=[sm, vm] + [hbm] * 6,
        out_specs=[vm] * 2,
        scratch_shapes=[
            vmem(96, NTH),
            vmem(192, NTH),
            vmem(128, 768),
            vmem(256, 128),
            vmem(2, 2, QUART + 16, PAIRS),
            vmem(2, 2, PAIRS, QUART),
            vmem(2, 2, QUART + 16, PAIRS),
            vmem(2, 2, PAIRS, QUART),
            vmem(2048, 128, dtype=F32),
            vmem(2048, 128, dtype=F32),
            vmem(128, 16, 128),
            vmem(128, 16, 128),
            vmem(PAIRS, PAIRS),
            vmem(PAIRS, PAIRS),
            vmem(PAIRS, 128, dtype=I32),
            vmem(PAIRS, 128, dtype=F32),
            vmem(2, 2, PAIRS, 256),
            vmem(2, 2, QUART, 128),
            vmem(128, 16, 128),
            vmem(128, 16, 128),
            vmem(2, NR, 16, 16, 128),
            vmem(2, NR, 16, 16, 128),
            vmem(128, 16, 128),
            vmem(192, 192),
            vmem(192, 192),
            vmem(192, NTH),
            dma((6,)),
        ]
        + [dma((2,))] * 10
        + [pltpu.SemaphoreType.REGULAR],
        compiler_params=pltpu.CompilerParams(
            collective_id=0, has_side_effects=True, vmem_limit_bytes=60 << 20
        ),
    )(
        order_slots, order_slots.reshape(8, 128), vel, tst,
        jnp.asarray(expand_table()), jnp.asarray(fold_table()), jnp.asarray(fwd), jnp.asarray(inv),
    )
    emf, der = pl.pallas_call(
        settle,
        out_shape=[jax.ShapeDtypeStruct((192, NTH), BF16)] * 2,
        in_specs=[vm] * 2,
        out_specs=[hbm] * 2,
        scratch_shapes=[dma((2, 6))],
    )(emf, der)
    shape = (1, 2, 3, 2, 16, NTH)
    return emf.reshape(shape), der.reshape(shape)


def solution(mesh):
    return jax.shard_map(
        per_device,
        mesh=mesh,
        in_specs=(P("rad", None, None, "ma", None), P("rad", None, None, None, "ma", None), P()),
        out_specs=(P("rad", None, None, None, "ma", None), P("rad", None, None, None, "ma", None)),
        check_vma=False,
    )
```

```python
import functools

import jax
import jax.numpy as jnp
import numpy as np
from jax import lax
from jax.experimental import pallas as pl
from jax.experimental.pallas import tpu as pltpu
from jax.sharding import PartitionSpec as P

MESH = pl.DeviceIdType.MESH
M = 1024
NTH = 1536
NPHI = 3072
QUART = NPHI // 4
PAIRS = M // 2
NR = 4
NMA = 64
F32 = jnp.float32
BF16 = jnp.bfloat16
I32 = jnp.int32
PB = 256
EMF_HOME = (False, True)


def cheb_matrix(level_count):
    levels_at = np.arange(level_count)
    points = np.cos(np.pi * levels_at / (level_count - 1))
    weights = np.where((levels_at == 0) | (levels_at == level_count - 1), 2.0, 1.0) * np.where(
        levels_at % 2 == 0, 1.0, -1.0
    )
    identity = np.eye(level_count)
    spread = points[:, None] - points[None, :] + identity
    offdiag = weights[:, None] / weights[None, :] / spread * (1.0 - identity)
    matrix = offdiag - identity * offdiag.sum(axis=1)[:, None]
    return np.asarray(matrix / level_count, dtype=np.float32)


DERIV = cheb_matrix(NR)


def phase_tables():
    r = np.arange(M // 2)
    p = np.arange(QUART + 1)
    fwd = np.zeros((2, 2, QUART + 16, M // 2), np.float32)
    inv = np.zeros((2, 2, M // 2, QUART), np.float32)
    for par, m in enumerate((2 * r, M - 1 - 2 * r)):
        q = (p[:, None] * m[None, :]) % NPHI
        ang = q.astype(np.float32) * np.float32(2.0 * np.pi / NPHI)
        for k, tab in enumerate((np.cos(ang), -np.sin(ang))):
            fwd[par, k, : QUART + 1] = tab
            inv[par, k] = tab[:QUART].T
    inv[:, :, :, 0] *= 0.5
    sign = np.where(r % 2 == 0, 1.0, -1.0)
    fwd[:, :, QUART] = 0.0
    fwd[0, 0, QUART] = sign
    fwd[1, 1, QUART] = sign
    return fwd.astype(jnp.bfloat16), inv.astype(jnp.bfloat16)


def expand_table():
    tab = np.zeros((3, 128, 256), np.float32)
    groups = []
    for f in range(2):
        for g, c in enumerate((1, 2, 0, 1)):
            groups.append((12 * (4 * f + g), c))
    b_first = 128 + 116
    for f in range(2):
        base = 3 + 3 * f
        for g, c in enumerate((2, 0, 1)):
            groups.append((128 + 12 * (4 * f + g), base + c))
        groups.append((b_first if f == 0 else 128 + 36, base + 1))
    for lane0, c in groups:
        for h in range(2):
            for v in range(6):
                lane = lane0 + h * 6 + v
                tab[0, c * 12 + h * 6 + v, lane] = 1
                tab[1, c * 12 + (1 - h) * 6 + v, lane] = 1
                tab[2, 108 + h * 9 + c, lane] = 1
    return np.concatenate(list(tab), axis=1).astype(jnp.bfloat16)


OUT_GROUPS = (0, 1, 2, 4, 5, 6)


def fold_table():
    tab = np.zeros((2, 128, 128), np.float32)
    for g, grp in enumerate(OUT_GROUPS):
        for h in range(2):
            for v in range(6):
                lane = grp * 12 + h * 6 + v
                tab[0, grp * 12 + (1 - h) * 6 + v, lane] = 1
                tab[1, lane, 96 + h * 6 + g] = 1
    return np.concatenate(list(tab), axis=0).astype(jnp.bfloat16)


def dot(a, b):
    return jnp.dot(a, b, preferred_element_type=F32)


def iota(shape, dim):
    return lax.broadcasted_iota(I32, shape, dim)


def onehot(cond):
    return jnp.where(cond, 1.0, 0.0).astype(BF16)


def cross(x):
    a, b = x[:, :128], x[:, 128:]
    return a * b - pltpu.roll(a, 116, 1) * pltpu.roll(b, 12, 1)


def kernel(
    slot_smem, slot_ref, vel_hbm, tst_hbm, exp_hbm, fold_hbm, fwd_hbm, inv_hbm,
    emf_hbm, der_hbm,
    emf_ref, der_ref, vel_ref, tst_ref, exp_ref, fold_ref, fwd_raw, inv_raw, fwd_tab, inv_tab, packed, turned, sendbuf, recvbuf,
    perm, permt, triple, sign, rhs, folded, outbuf, backbuf, radbuf, dersend, derbuf, quse, qback, rows,
    load_sem, f_send, f_recv, b_send, b_recv, y_send, y_recv, d_send, d_recv, own_send, e_send, out_sem, ready,
):
    me = lax.axis_index("ma")
    lev = lax.axis_index("rad")

    barrier = pltpu.get_barrier_semaphore()

    def greet(step, carry):
        pl.semaphore_signal(
            barrier, inc=1, device_id=(lev, lax.rem(me + step, NMA)), device_id_type=MESH
        )
        return carry

    loads = [
        pltpu.make_async_copy(src, dst, load_sem.at[i])
        for i, (src, dst) in enumerate(
            (
                (vel_hbm, vel_ref), (tst_hbm, tst_ref), (fwd_hbm, fwd_raw), (inv_hbm, inv_raw),
                (exp_hbm, exp_ref), (fold_hbm, fold_ref),
            )
        )
    ]
    loads[0].start()
    loads[1].start()
    lax.fori_loop(1, NMA, greet, 0)
    for step in range(1, NR):
        pl.semaphore_signal(barrier, inc=1, device_id=(lax.rem(lev + step, NR), me), device_id_type=MESH)
    for load in loads[2:]:
        load.start()

    firsts = [slot_smem[me * 16 + 2 * i] for i in range(8)]

    def spread(pair, shape):
        out = jnp.full(shape, firsts[7], I32)
        for i in range(7):
            out = jnp.where(pair == i, firsts[i], out)
        return out

    def onehot_rows(dim):
        here = iota((192, 192), dim)
        first = spread(here & 7, (192, 192))
        slot = (here & ~31) + ((here & 8) << 1) + 2 * (here & 7) + (((here >> 4) ^ first) & 1)
        return onehot(slot == iota((192, 192), 1 - dim))

    quse[...] = onehot_rows(0)
    qback[...] = onehot_rows(1)
    lane = iota((16, 128), 1)
    first = spread(iota((16, 128), 0) & 7, (16, 128))
    even = jnp.where((first & 1) == 0, first, (M - 1) - first)
    odd = (M - 1) - even

    def masks(v):
        out = []
        for h in range(2):
            j = 128 * v + lane
            near = (j + 1) if h == 0 else (768 - j)
            out.append((even * NTH <= 2 * M * near, odd * NTH <= 2 * M * near))
        return out

    loads[0].wait()
    loads[1].wait()
    left = {}
    for w in range(3):
        halves = []
        for h in range(2):
            cols = slice(768 * h + 256 * w, 768 * h + 256 * w + 256)
            halves.append(
                (dot(quse[0:96, 0:96], vel_ref[:, cols]), dot(quse[...], tst_ref[:, cols]))
            )
        for vv in range(2):
            v = 2 * w + vv
            live = masks(v)
            for c in range(9):
                xe, xo = [], []
                for h in range(2):
                    src = halves[h][0] if c < 3 else halves[h][1]
                    row = 32 * (c if c < 3 else c - 3)
                    xe.append(src[row : row + 16, 128 * vv : 128 * vv + 128])
                    xo.append(src[row + 16 : row + 32, 128 * vv : 128 * vv + 128])
                for h in range(2):
                    spot = (c * 12 + h * 6 + v) * 16
                    packed[spot : spot + 16, :] = jnp.where(live[h][0], xe[h], xo[1 - h])
                    rest = jnp.where(live[h][1] & live[1 - h][0], xo[h], 0.0)
                    left[h, c] = rest if v == 0 else left[h, c] + rest
    for h in range(2):
        for c in range(9):
            spot = (108 + h * 9 + c) * 16
            packed[spot : spot + 16, :] = left[h, c]
    packed[126 * 16 : 128 * 16, :] = jnp.zeros((32, 128), F32)
    for row in range(16):
        turned[pl.ds(row, 128, stride=16), :] = packed[pl.ds(row, 128, stride=16), :].T
    sendbuf[...] = turned[...].astype(BF16).reshape(128, 16, 128)

    pl.semaphore_wait(barrier, NMA - 1 + NR - 1)
    for step in range(1, NR):
        pl.semaphore_signal(ready, inc=1, device_id=(lax.rem(lev + step, NR), me), device_id_type=MESH)

    def all_to_all(src, dst, ssem, rsem, u):
        def one(step, carry):
            to = lax.rem(me + step, NMA)
            pltpu.make_async_remote_copy(
                src_ref=src.at[u * NMA + to],
                dst_ref=dst.at[u * NMA + me],
                send_sem=ssem.at[u],
                recv_sem=rsem.at[u],
                device_id=(lev, to),
                device_id_type=MESH,
            ).start()
            return carry

        pltpu.make_async_copy(src.at[u * NMA + me], dst.at[u * NMA + me], rsem.at[u]).start()
        lax.fori_loop(1, NMA, one, 0)

    deriver = me // 16
    place = lax.rem(me, 16)

    def to_deriver(u, b):
        def one(step, carry):
            to = 32 * b + lax.rem(me + step, 32)

            @pl.when(to != me)
            def _():
                pltpu.make_async_remote_copy(
                    src_ref=outbuf.at[u * NMA + to],
                    dst_ref=radbuf.at[u, lev, place],
                    send_sem=y_send.at[u],
                    recv_sem=y_recv.at[u],
                    device_id=(deriver, to),
                    device_id_type=MESH,
                ).start()

            return carry

        lax.fori_loop(0, 32, one, 0)

    def own_to_deriver(u):
        @pl.when(deriver == lev)
        def _():
            pltpu.make_async_copy(outbuf.at[u * NMA + me], radbuf.at[u, lev, place], y_recv.at[u]).start()

        @pl.when(deriver != lev)
        def _():
            pltpu.make_async_remote_copy(
                src_ref=outbuf.at[u * NMA + me],
                dst_ref=radbuf.at[u, lev, place],
                send_sem=own_send.at[u],
                recv_sem=y_recv.at[u],
                device_id=(deriver, me),
                device_id_type=MESH,
            ).start()

    def wait_bytes(ref, sem):
        pltpu.make_async_copy(ref, ref, sem).wait()

    for u in range(2):
        all_to_all(sendbuf, recvbuf, f_send, f_recv, u)

    slots = slot_ref[...]
    rank = jnp.where((slots & 1) == 0, slots, (M - 1) - slots) >> 1
    high = (rank >> 4).astype(F32).astype(BF16)
    low = (rank & 15).astype(F32).astype(BF16)
    at_row, at_lane = iota((128, 128), 0), iota((128, 128), 1)
    parts = []
    for side in range(2):
        pick = onehot(at_row == 2 * (at_lane - 64 * side))
        parts.append(dot(high, pick) * 16.0 + dot(low, pick))
    keys = jnp.concatenate([parts[0][2 * b : 2 * b + 1] + parts[1][2 * b + 1 : 2 * b + 2] for b in range(4)] * 2, axis=0)
    keys_t = keys.T
    for b in range(4):
        blk = slice(128 * b, 128 * b + 128)
        perm[:, blk] = onehot(keys[b : b + 1, :] == iota((PAIRS, 128), 0).astype(F32))
        column = keys_t[:, b : b + 1]
        permt[blk, :] = onehot(column == iota((128, PAIRS), 1).astype(F32))
        wide = jnp.broadcast_to(column, (128, 128)).astype(I32)
        triple[blk, :] = 3 * wide
        sign[blk, :] = (1 - 2 * (wide & 1)).astype(F32)

    for load in loads[2:]:
        load.wait()

    def build(i, carry):
        for par in range(2):
            for k in range(2):
                spot = pl.ds(pl.multiple_of(i * 256, 256), 256)
                fwd_tab[par, k, spot, :] = dot(fwd_raw[par, k, spot, :], perm[...]).astype(BF16)
                inv_tab[par, k, :, spot] = dot(permt[...], inv_raw[par, k, :, spot]).astype(BF16)
        return carry

    lax.fori_loop(0, QUART // 256, build, 0)
    for par in range(2):
        for k in range(2):
            last = slice(QUART, QUART + 16)
            fwd_tab[par, k, last, :] = dot(fwd_raw[par, k, last, :], perm[...]).astype(BF16)

    def near_of(lane_id, u):
        l12 = jnp.where(lane_id >= 116, lane_id - 116, lax.rem(lane_id, 12))
        h = l12 >= 6
        v = jnp.where(h, l12 - 6, l12)
        j = 128 * v + 64 * u + me
        return jnp.where(h, 768 - j, j + 1)

    scale = NPHI ** (-0.5)

    for u in range(2):
        lane1 = iota((1, 128), 1)
        near = near_of(lane1, u)
        main = lane1 < 96
        own_top, far_top, odd_low = 2 * near, 1538 - 2 * near, 1535 - 2 * near
        wait_bytes(recvbuf.at[pl.ds(u * NMA, NMA)], f_recv.at[u])
        for b in range(4):
            blk = slice(128 * b, 128 * b + 128)
            got = recvbuf[u * NMA + 16 * b : u * NMA + 16 * b + 16].reshape(256, 128)
            wide = dot(got, exp_ref[...]).reshape(16, 2, 8, 768)
            tri = triple[blk, :]
            own_live = tri <= own_top
            far_live = tri <= far_top
            odd_live = tri >= odd_low
            for k in range(2):
                part = wide[:, k].reshape(128, 768)
                for t in range(2):
                    cols = slice(128 * t, 128 * t + 128)
                    same, swap, rest = (part[:, 256 * i + 128 * t : 256 * i + 128 * t + 128] for i in range(3))
                    rhs[0, k, blk, cols] = jnp.where(own_live, same, 0.0).astype(BF16)
                    other = jnp.where(far_live, rest, swap)
                    rhs[1, k, blk, cols] = jnp.where(odd_live, other, 0.0).astype(BF16)

        def longitudes(i, carry):
            spot = pl.ds(pl.multiple_of(i * PB, PB), PB)
            ce, se, co, so = (
                dot(fwd_tab[par, k, spot, :], rhs[par, k]) for par in range(2) for k in range(2)
            )
            ve, vo = ce + se, co + so
            me_, mo = ce - se, so - co
            e1, e2 = cross(ve + vo), cross(ve - vo)
            e3, e4 = cross(me_ + mo), cross(me_ - mo)
            us, ws, um, wm = e1 + e2, e1 - e2, e3 + e4, e3 - e4
            folded[0, 0, spot, :] = (us + um).astype(BF16)
            folded[0, 1, spot, :] = (us - um).astype(BF16)
            folded[1, 0, spot, :] = (ws - wm).astype(BF16)
            folded[1, 1, spot, :] = (ws + wm).astype(BF16)
            return carry

        lax.fori_loop(0, QUART // PB, longitudes, 0, unroll=True)
        last = slice(QUART, QUART + 16)
        ve, vo = (
            dot(fwd_tab[par, 0, last, :], rhs[par, 0]) + dot(fwd_tab[par, 1, last, :], rhs[par, 1])
            for par in range(2)
        )
        e1, e2 = cross(ve + vo), cross(ve - vo)
        quarter = ((e1 + e2)[0:1], (e1 - e2)[0:1])

        for b in range(2):
            blk = slice(256 * b, 256 * b + 256)
            tri = triple[blk, :]
            own_live = (tri <= own_top) & main
            both_live = (tri >= odd_low) & (tri <= far_top) & main
            out = []
            for k in range(2):
                se = dot(inv_tab[0, k, blk, :], folded[0, k])
                so = dot(inv_tab[1, k, blk, :], folded[1, k])
                if k == 0:
                    se = se + sign[blk, :] * quarter[0]
                else:
                    so = so + sign[blk, :] * quarter[1]
                so = so * scale
                rest = jnp.where(both_live, so, 0.0)
                moved = dot(jnp.concatenate([so, rest], axis=1).astype(BF16), fold_ref[...])
                out.append(jnp.where(own_live, se * scale, moved).reshape(32, 1, 8, 128))
            outbuf[u * NMA + 32 * b : u * NMA + 32 * b + 32] = (
                jnp.concatenate(out, axis=1).reshape(32, 16, 128).astype(BF16)
            )
            if u == 0 and b == 0:
                pl.semaphore_wait(ready, NR - 1)
            to_deriver(u, b)
        own_to_deriver(u)
        if EMF_HOME[u]:
            all_to_all(outbuf, backbuf, b_send, b_recv, u)

    def rad_derive(u):
        wait_bytes(radbuf.at[u], y_recv.at[u])
        vals = [radbuf[u, k].astype(F32) for k in range(NR)]
        for i in range(NR):
            acc = vals[0] * float(DERIV[i, 0])
            for k in range(1, NR):
                acc = acc + vals[k] * float(DERIV[i, k])
            dersend[u, i] = acc.astype(BF16)
        for step in range(1, NR):
            to = lax.rem(lev + step, NR)
            pltpu.make_async_remote_copy(
                src_ref=dersend.at[u, to],
                dst_ref=derbuf.at[pl.ds(u * NMA + 16 * lev, 16)],
                send_sem=d_send.at[u],
                recv_sem=d_recv.at[u],
                device_id=(to, me),
                device_id_type=MESH,
            ).start()
        pltpu.make_async_copy(
            dersend.at[u, lev], derbuf.at[pl.ds(u * NMA + 16 * lev, 16)], d_recv.at[u]
        ).start()
        if not EMF_HOME[u]:
            for step in range(1, NR):
                to = lax.rem(lev + step, NR)
                pltpu.make_async_remote_copy(
                    src_ref=radbuf.at[u, to],
                    dst_ref=backbuf.at[pl.ds(u * NMA + 16 * lev, 16)],
                    send_sem=e_send.at[u],
                    recv_sem=b_recv.at[u],
                    device_id=(to, me),
                    device_id_type=MESH,
                ).start()
            pltpu.make_async_copy(
                radbuf.at[u, lev], backbuf.at[pl.ds(u * NMA + 16 * lev, 16)], b_recv.at[u]
            ).start()

    def unpack(buf, out_ref, out_hbm, sem):
        turned[...] = buf[...].astype(F32).reshape(2048, 128)
        for row in range(16):
            packed[pl.ds(row, 128, stride=16), :] = turned[pl.ds(row, 128, stride=16), :].T
        for v in range(6):
            live = masks(v)
            for g, grp in enumerate(OUT_GROUPS):
                half = []
                for h in range(2):
                    spot = (grp * 12 + h * 6 + v) * 16
                    half.append(packed[spot : spot + 16, :])
                for h in range(2):
                    spot = (96 + h * 6 + g) * 16
                    rest = packed[spot : spot + 16, :]
                    cols = slice(768 * h + 128 * v, 768 * h + 128 * v + 128)
                    rows[32 * g : 32 * g + 16, cols] = jnp.where(live[h][0], half[h], 0.0).astype(BF16)
                    other = jnp.where(live[1 - h][0], rest, half[1 - h])
                    rows[32 * g + 16 : 32 * g + 32, cols] = jnp.where(live[h][1], other, 0.0).astype(BF16)
        for w in range(6):
            cols = pl.ds(256 * w, 256)
            out_ref[:, cols] = dot(qback[...], rows[:, cols]).astype(BF16)
            pltpu.make_async_copy(out_ref.at[:, cols], out_hbm.at[:, cols], sem).start()

    for u in range(2):
        rad_derive(u)
    for u in range(2):
        wait_bytes(backbuf.at[pl.ds(u * NMA, NMA)], b_recv.at[u])
    unpack(backbuf, emf_ref, emf_hbm, out_sem.at[0])
    for u in range(2):
        wait_bytes(derbuf.at[pl.ds(u * NMA, NMA)], d_recv.at[u])
    unpack(derbuf, der_ref, der_hbm, out_sem.at[1])

    for u in range(2):
        wait_bytes(sendbuf.at[pl.ds(0, NMA - 1)], f_send.at[u])
        wait_bytes(outbuf.at[pl.ds(0, NMA - 1)], y_send.at[u])

        @pl.when(deriver != lev)
        def _():
            wait_bytes(outbuf.at[0], own_send.at[u])

        wait_bytes(dersend.at[u, pl.ds(0, NR - 1)], d_send.at[u])
        if EMF_HOME[u]:
            wait_bytes(outbuf.at[pl.ds(0, NMA - 1)], b_send.at[u])
        else:
            wait_bytes(radbuf.at[u, pl.ds(0, NR - 1)], e_send.at[u])
    wait_bytes(emf_ref, out_sem.at[0])
    wait_bytes(der_ref, out_sem.at[1])


def settle(emf_in, der_in, emf_out, der_out, held, in_sem, out_sem):
    loads, stores = [], []
    for i, (src, dst) in enumerate(((emf_in, emf_out), (der_in, der_out))):
        for part in range(3):
            blk = pl.ds(part * 64, 64)
            loads.append(pltpu.make_async_copy(src.at[blk], held.at[i, blk], in_sem.at[i, part]))
            stores.append(pltpu.make_async_copy(held.at[i, blk], dst.at[blk], out_sem.at[i, part]))
    for load in loads:
        load.start()
    for load, store in zip(loads, stores):
        load.wait()
        store.start()
    for store in stores:
        store.wait()


def per_device(velocity, test_fields, order_slots):
    vel = velocity.reshape(3 * 2 * 16, NTH)
    tst = test_fields.reshape(6 * 2 * 16, NTH)
    fwd, inv = phase_tables()
    vm = pl.BlockSpec(memory_space=pltpu.VMEM)
    sm = pl.BlockSpec(memory_space=pltpu.SMEM)
    hbm = pl.BlockSpec(memory_space=pl.ANY)
    dma = pltpu.SemaphoreType.DMA

    def vmem(*shape, dtype=BF16):
        return pltpu.VMEM(shape, dtype)

    emf, der = pl.pallas_call(
        kernel,
        out_shape=[jax.ShapeDtypeStruct((192, NTH), BF16)] * 2,
        in_specs=[sm, vm] + [hbm] * 6,
        out_specs=[hbm] * 2,
        scratch_shapes=[
            vmem(192, NTH),
            vmem(192, NTH),
            vmem(96, NTH),
            vmem(192, NTH),
            vmem(128, 768),
            vmem(256, 128),
            vmem(2, 2, QUART + 16, PAIRS),
            vmem(2, 2, PAIRS, QUART),
            vmem(2, 2, QUART + 16, PAIRS),
            vmem(2, 2, PAIRS, QUART),
            vmem(2048, 128, dtype=F32),
            vmem(2048, 128, dtype=F32),
            vmem(128, 16, 128),
            vmem(128, 16, 128),
            vmem(PAIRS, PAIRS),
            vmem(PAIRS, PAIRS),
            vmem(PAIRS, 128, dtype=I32),
            vmem(PAIRS, 128, dtype=F32),
            vmem(2, 2, PAIRS, 256),
            vmem(2, 2, QUART, 128),
            vmem(128, 16, 128),
            vmem(128, 16, 128),
            vmem(2, NR, 16, 16, 128),
            vmem(2, NR, 16, 16, 128),
            vmem(128, 16, 128),
            vmem(192, 192),
            vmem(192, 192),
            vmem(192, NTH),
            dma((6,)),
        ]
        + [dma((2,))] * 11
        + [pltpu.SemaphoreType.REGULAR],
        compiler_params=pltpu.CompilerParams(
            collective_id=0, has_side_effects=True, vmem_limit_bytes=60 << 20
        ),
    )(
        order_slots, order_slots.reshape(8, 128), vel, tst,
        jnp.asarray(expand_table()), jnp.asarray(fold_table()), jnp.asarray(fwd), jnp.asarray(inv),
    )
    emf, der = pl.pallas_call(
        settle,
        out_shape=[jax.ShapeDtypeStruct((192, NTH), BF16)] * 2,
        in_specs=[hbm] * 2,
        out_specs=[hbm] * 2,
        scratch_shapes=[vmem(2, 192, NTH), dma((2, 3)), dma((2, 3))],
    )(emf, der)
    shape = (1, 2, 3, 2, 16, NTH)
    return emf.reshape(shape), der.reshape(shape)


def solution(mesh):
    return jax.shard_map(
        per_device,
        mesh=mesh,
        in_specs=(P("rad", None, None, "ma", None), P("rad", None, None, None, "ma", None), P()),
        out_specs=(P("rad", None, None, None, "ma", None), P("rad", None, None, None, "ma", None)),
        check_vma=False,
    )
```

```python
import functools

import jax
import jax.numpy as jnp
import numpy as np
from jax import lax
from jax.experimental import pallas as pl
from jax.experimental.pallas import tpu as pltpu
from jax.sharding import PartitionSpec as P

MESH = pl.DeviceIdType.MESH
M = 1024
NTH = 1536
NPHI = 3072
QUART = NPHI // 4
PAIRS = M // 2
NR = 4
NMA = 64
F32 = jnp.float32
BF16 = jnp.bfloat16
I32 = jnp.int32
PB = 384
EMF_HOME = (False, True)


def cheb_matrix(level_count):
    levels_at = np.arange(level_count)
    points = np.cos(np.pi * levels_at / (level_count - 1))
    weights = np.where((levels_at == 0) | (levels_at == level_count - 1), 2.0, 1.0) * np.where(
        levels_at % 2 == 0, 1.0, -1.0
    )
    identity = np.eye(level_count)
    spread = points[:, None] - points[None, :] + identity
    offdiag = weights[:, None] / weights[None, :] / spread * (1.0 - identity)
    matrix = offdiag - identity * offdiag.sum(axis=1)[:, None]
    return np.asarray(matrix / level_count, dtype=np.float32)


DERIV = cheb_matrix(NR)


def phase_tables():
    r = np.arange(M // 2)
    p = np.arange(QUART + 1)
    fwd = np.zeros((2, 2, QUART + 16, M // 2), np.float32)
    inv = np.zeros((2, 2, M // 2, QUART), np.float32)
    for par, m in enumerate((2 * r, M - 1 - 2 * r)):
        q = (p[:, None] * m[None, :]) % NPHI
        ang = q.astype(np.float32) * np.float32(2.0 * np.pi / NPHI)
        for k, tab in enumerate((np.cos(ang), -np.sin(ang))):
            fwd[par, k, : QUART + 1] = tab
            inv[par, k] = tab[:QUART].T
    inv[:, :, :, 0] *= 0.5
    sign = np.where(r % 2 == 0, 1.0, -1.0)
    fwd[:, :, QUART] = 0.0
    fwd[0, 0, QUART] = sign
    fwd[1, 1, QUART] = sign
    return fwd.astype(jnp.bfloat16), inv.astype(jnp.bfloat16)


def expand_table():
    tab = np.zeros((3, 128, 256), np.float32)
    groups = []
    for f in range(2):
        for g, c in enumerate((1, 2, 0, 1)):
            groups.append((12 * (4 * f + g), c))
    b_first = 128 + 116
    for f in range(2):
        base = 3 + 3 * f
        for g, c in enumerate((2, 0, 1)):
            groups.append((128 + 12 * (4 * f + g), base + c))
        groups.append((b_first if f == 0 else 128 + 36, base + 1))
    for lane0, c in groups:
        for h in range(2):
            for v in range(6):
                lane = lane0 + h * 6 + v
                tab[0, c * 12 + h * 6 + v, lane] = 1
                tab[1, c * 12 + (1 - h) * 6 + v, lane] = 1
                tab[2, 108 + h * 9 + c, lane] = 1
    return np.concatenate(list(tab), axis=1).astype(jnp.bfloat16)


OUT_GROUPS = (0, 1, 2, 4, 5, 6)


def fold_table():
    tab = np.zeros((2, 128, 128), np.float32)
    for g, grp in enumerate(OUT_GROUPS):
        for h in range(2):
            for v in range(6):
                lane = grp * 12 + h * 6 + v
                tab[0, grp * 12 + (1 - h) * 6 + v, lane] = 1
                tab[1, lane, 96 + h * 6 + g] = 1
    return np.concatenate(list(tab), axis=0).astype(jnp.bfloat16)


def dot(a, b):
    return jnp.dot(a, b, preferred_element_type=F32)


def iota(shape, dim):
    return lax.broadcasted_iota(I32, shape, dim)


def onehot(cond):
    return jnp.where(cond, 1.0, 0.0).astype(BF16)


def cross(x):
    a, b = x[:, :128], x[:, 128:]
    return a * b - pltpu.roll(a, 116, 1) * pltpu.roll(b, 12, 1)


def kernel(
    slot_smem, slot_ref, vel_hbm, tst_hbm, exp_hbm, fold_hbm, fwd_hbm, inv_hbm,
    emf_hbm, der_hbm,
    emf_ref, der_ref, vel_ref, tst_ref, exp_ref, fold_ref, fwd_raw, inv_raw, fwd_tab, inv_tab, packed, turned, sendbuf, recvbuf,
    perm, permt, triple, sign, rhs, folded, outbuf, backbuf, radbuf, dersend, derbuf, quse, qback, rows,
    load_sem, f_send, f_recv, b_send, b_recv, y_send, y_recv, d_send, d_recv, own_send, e_send, out_sem, ready,
):
    me = lax.axis_index("ma")
    lev = lax.axis_index("rad")

    barrier = pltpu.get_barrier_semaphore()

    def greet(step, carry):
        pl.semaphore_signal(
            barrier, inc=1, device_id=(lev, lax.rem(me + step, NMA)), device_id_type=MESH
        )
        return carry

    loads = [
        pltpu.make_async_copy(src, dst, load_sem.at[i])
        for i, (src, dst) in enumerate(
            (
                (vel_hbm, vel_ref), (tst_hbm, tst_ref), (fwd_hbm, fwd_raw), (inv_hbm, inv_raw),
                (exp_hbm, exp_ref), (fold_hbm, fold_ref),
            )
        )
    ]
    loads[0].start()
    loads[1].start()
    lax.fori_loop(1, NMA, greet, 0)
    for step in range(1, NR):
        pl.semaphore_signal(barrier, inc=1, device_id=(lax.rem(lev + step, NR), me), device_id_type=MESH)
    for load in loads[2:]:
        load.start()

    firsts = [slot_smem[me * 16 + 2 * i] for i in range(8)]

    def spread(pair, shape):
        out = jnp.full(shape, firsts[7], I32)
        for i in range(7):
            out = jnp.where(pair == i, firsts[i], out)
        return out

    def onehot_rows(dim):
        here = iota((192, 192), dim)
        first = spread(here & 7, (192, 192))
        slot = (here & ~31) + ((here & 8) << 1) + 2 * (here & 7) + (((here >> 4) ^ first) & 1)
        return onehot(slot == iota((192, 192), 1 - dim))

    quse[...] = onehot_rows(0)
    qback[...] = onehot_rows(1)
    lane = iota((16, 128), 1)
    first = spread(iota((16, 128), 0) & 7, (16, 128))
    even = jnp.where((first & 1) == 0, first, (M - 1) - first)
    odd = (M - 1) - even

    def masks(v):
        out = []
        for h in range(2):
            j = 128 * v + lane
            near = (j + 1) if h == 0 else (768 - j)
            out.append((even * NTH <= 2 * M * near, odd * NTH <= 2 * M * near))
        return out

    loads[0].wait()
    loads[1].wait()
    left = {}
    for w in range(3):
        halves = []
        for h in range(2):
            cols = slice(768 * h + 256 * w, 768 * h + 256 * w + 256)
            halves.append(
                (dot(quse[0:96, 0:96], vel_ref[:, cols]), dot(quse[...], tst_ref[:, cols]))
            )
        for vv in range(2):
            v = 2 * w + vv
            live = masks(v)
            for c in range(9):
                xe, xo = [], []
                for h in range(2):
                    src = halves[h][0] if c < 3 else halves[h][1]
                    row = 32 * (c if c < 3 else c - 3)
                    xe.append(src[row : row + 16, 128 * vv : 128 * vv + 128])
                    xo.append(src[row + 16 : row + 32, 128 * vv : 128 * vv + 128])
                for h in range(2):
                    spot = (c * 12 + h * 6 + v) * 16
                    packed[spot : spot + 16, :] = jnp.where(live[h][0], xe[h], xo[1 - h])
                    rest = jnp.where(live[h][1] & live[1 - h][0], xo[h], 0.0)
                    left[h, c] = rest if v == 0 else left[h, c] + rest
    for h in range(2):
        for c in range(9):
            spot = (108 + h * 9 + c) * 16
            packed[spot : spot + 16, :] = left[h, c]
    packed[126 * 16 : 128 * 16, :] = jnp.zeros((32, 128), F32)
    for row in range(16):
        turned[pl.ds(row, 128, stride=16), :] = packed[pl.ds(row, 128, stride=16), :].T
    sendbuf[...] = turned[...].astype(BF16).reshape(128, 16, 128)

    pl.semaphore_wait(barrier, NMA - 1 + NR - 1)
    for step in range(1, NR):
        pl.semaphore_signal(ready, inc=1, device_id=(lax.rem(lev + step, NR), me), device_id_type=MESH)

    def all_to_all(src, dst, ssem, rsem, u):
        def one(step, carry):
            to = lax.rem(me + step, NMA)
            pltpu.make_async_remote_copy(
                src_ref=src.at[u * NMA + to],
                dst_ref=dst.at[u * NMA + me],
                send_sem=ssem.at[u],
                recv_sem=rsem.at[u],
                device_id=(lev, to),
                device_id_type=MESH,
            ).start()
            return carry

        pltpu.make_async_copy(src.at[u * NMA + me], dst.at[u * NMA + me], rsem.at[u]).start()
        lax.fori_loop(1, NMA, one, 0)

    deriver = me // 16
    place = lax.rem(me, 16)

    def to_deriver(u, b):
        def one(step, carry):
            to = 32 * b + lax.rem(me + step, 32)

            @pl.when(to != me)
            def _():
                pltpu.make_async_remote_copy(
                    src_ref=outbuf.at[u * NMA + to],
                    dst_ref=radbuf.at[u, lev, place],
                    send_sem=y_send.at[u],
                    recv_sem=y_recv.at[u],
                    device_id=(deriver, to),
                    device_id_type=MESH,
                ).start()

            return carry

        lax.fori_loop(0, 32, one, 0)

    def own_to_deriver(u):
        @pl.when(deriver == lev)
        def _():
            pltpu.make_async_copy(outbuf.at[u * NMA + me], radbuf.at[u, lev, place], y_recv.at[u]).start()

        @pl.when(deriver != lev)
        def _():
            pltpu.make_async_remote_copy(
                src_ref=outbuf.at[u * NMA + me],
                dst_ref=radbuf.at[u, lev, place],
                send_sem=own_send.at[u],
                recv_sem=y_recv.at[u],
                device_id=(deriver, me),
                device_id_type=MESH,
            ).start()

    def wait_bytes(ref, sem):
        pltpu.make_async_copy(ref, ref, sem).wait()

    for u in range(2):
        all_to_all(sendbuf, recvbuf, f_send, f_recv, u)

    slots = slot_ref[...]
    rank = jnp.where((slots & 1) == 0, slots, (M - 1) - slots) >> 1
    high = (rank >> 4).astype(F32).astype(BF16)
    low = (rank & 15).astype(F32).astype(BF16)
    at_row, at_lane = iota((128, 128), 0), iota((128, 128), 1)
    parts = []
    for side in range(2):
        pick = onehot(at_row == 2 * (at_lane - 64 * side))
        parts.append(dot(high, pick) * 16.0 + dot(low, pick))
    keys = jnp.concatenate([parts[0][2 * b : 2 * b + 1] + parts[1][2 * b + 1 : 2 * b + 2] for b in range(4)] * 2, axis=0)
    keys_t = keys.T
    for b in range(4):
        blk = slice(128 * b, 128 * b + 128)
        perm[:, blk] = onehot(keys[b : b + 1, :] == iota((PAIRS, 128), 0).astype(F32))
        column = keys_t[:, b : b + 1]
        permt[blk, :] = onehot(column == iota((128, PAIRS), 1).astype(F32))
        wide = jnp.broadcast_to(column, (128, 128)).astype(I32)
        triple[blk, :] = 3 * wide
        sign[blk, :] = (1 - 2 * (wide & 1)).astype(F32)

    for load in loads[2:]:
        load.wait()

    def build(i, carry):
        for par in range(2):
            for k in range(2):
                spot = pl.ds(pl.multiple_of(i * 256, 256), 256)
                fwd_tab[par, k, spot, :] = dot(fwd_raw[par, k, spot, :], perm[...]).astype(BF16)
                inv_tab[par, k, :, spot] = dot(permt[...], inv_raw[par, k, :, spot]).astype(BF16)
        return carry

    lax.fori_loop(0, QUART // 256, build, 0)
    for par in range(2):
        for k in range(2):
            last = slice(QUART, QUART + 16)
            fwd_tab[par, k, last, :] = dot(fwd_raw[par, k, last, :], perm[...]).astype(BF16)

    def near_of(lane_id, u):
        l12 = jnp.where(lane_id >= 116, lane_id - 116, lax.rem(lane_id, 12))
        h = l12 >= 6
        v = jnp.where(h, l12 - 6, l12)
        j = 128 * v + 64 * u + me
        return jnp.where(h, 768 - j, j + 1)

    scale = NPHI ** (-0.5)

    for u in range(2):
        lane1 = iota((1, 128), 1)
        near = near_of(lane1, u)
        main = lane1 < 96
        own_top, far_top, odd_low = 2 * near, 1538 - 2 * near, 1535 - 2 * near
        wait_bytes(recvbuf.at[pl.ds(u * NMA, NMA)], f_recv.at[u])
        for b in range(4):
            blk = slice(128 * b, 128 * b + 128)
            got = recvbuf[u * NMA + 16 * b : u * NMA + 16 * b + 16].reshape(256, 128)
            wide = dot(got, exp_ref[...]).reshape(16, 2, 8, 768)
            tri = triple[blk, :]
            own_live = tri <= own_top
            far_live = tri <= far_top
            odd_live = tri >= odd_low
            for k in range(2):
                part = wide[:, k].reshape(128, 768)
                for t in range(2):
                    cols = slice(128 * t, 128 * t + 128)
                    same, swap, rest = (part[:, 256 * i + 128 * t : 256 * i + 128 * t + 128] for i in range(3))
                    rhs[0, k, blk, cols] = jnp.where(own_live, same, 0.0).astype(BF16)
                    other = jnp.where(far_live, rest, swap)
                    rhs[1, k, blk, cols] = jnp.where(odd_live, other, 0.0).astype(BF16)

        def longitudes(i, carry):
            spot = pl.ds(pl.multiple_of(i * PB, PB), PB)
            ce, se, co, so = (
                dot(fwd_tab[par, k, spot, :], rhs[par, k]) for par in range(2) for k in range(2)
            )
            ve, vo = ce + se, co + so
            me_, mo = ce - se, so - co
            e1, e2 = cross(ve + vo), cross(ve - vo)
            e3, e4 = cross(me_ + mo), cross(me_ - mo)
            us, ws, um, wm = e1 + e2, e1 - e2, e3 + e4, e3 - e4
            folded[0, 0, spot, :] = (us + um).astype(BF16)
            folded[0, 1, spot, :] = (us - um).astype(BF16)
            folded[1, 0, spot, :] = (ws - wm).astype(BF16)
            folded[1, 1, spot, :] = (ws + wm).astype(BF16)
            return carry

        lax.fori_loop(0, QUART // PB, longitudes, 0, unroll=True)
        last = slice(QUART, QUART + 16)
        ve, vo = (
            dot(fwd_tab[par, 0, last, :], rhs[par, 0]) + dot(fwd_tab[par, 1, last, :], rhs[par, 1])
            for par in range(2)
        )
        e1, e2 = cross(ve + vo), cross(ve - vo)
        quarter = ((e1 + e2)[0:1], (e1 - e2)[0:1])

        for b in range(2):
            blk = slice(256 * b, 256 * b + 256)
            tri = triple[blk, :]
            own_live = (tri <= own_top) & main
            both_live = (tri >= odd_low) & (tri <= far_top) & main
            out = []
            for k in range(2):
                se = dot(inv_tab[0, k, blk, :], folded[0, k])
                so = dot(inv_tab[1, k, blk, :], folded[1, k])
                if k == 0:
                    se = se + sign[blk, :] * quarter[0]
                else:
                    so = so + sign[blk, :] * quarter[1]
                so = so * scale
                rest = jnp.where(both_live, so, 0.0)
                moved = dot(jnp.concatenate([so, rest], axis=1).astype(BF16), fold_ref[...])
                out.append(jnp.where(own_live, se * scale, moved).reshape(32, 1, 8, 128))
            outbuf[u * NMA + 32 * b : u * NMA + 32 * b + 32] = (
                jnp.concatenate(out, axis=1).reshape(32, 16, 128).astype(BF16)
            )
            if u == 0 and b == 0:
                pl.semaphore_wait(ready, NR - 1)
            to_deriver(u, b)
        own_to_deriver(u)
        if EMF_HOME[u]:

            @pl.when(deriver != lev)
            def _():
                all_to_all(outbuf, backbuf, b_send, b_recv, u)

    def rad_derive(u):
        wait_bytes(radbuf.at[u], y_recv.at[u])
        vals = [radbuf[u, k].astype(F32) for k in range(NR)]
        for i in range(NR):
            acc = vals[0] * float(DERIV[i, 0])
            for k in range(1, NR):
                acc = acc + vals[k] * float(DERIV[i, k])
            dersend[u, i] = acc.astype(BF16)
        for step in range(1, NR):
            to = lax.rem(lev + step, NR)
            pltpu.make_async_remote_copy(
                src_ref=dersend.at[u, to],
                dst_ref=derbuf.at[pl.ds(u * NMA + 16 * lev, 16)],
                send_sem=d_send.at[u],
                recv_sem=d_recv.at[u],
                device_id=(to, me),
                device_id_type=MESH,
            ).start()
        pltpu.make_async_copy(
            dersend.at[u, lev], derbuf.at[pl.ds(u * NMA + 16 * lev, 16)], d_recv.at[u]
        ).start()
        if EMF_HOME[u]:
            pltpu.make_async_copy(
                radbuf.at[u, lev], backbuf.at[pl.ds(u * NMA + 16 * lev, 16)], b_recv.at[u]
            ).start()
        else:
            for step in range(1, NR):
                to = lax.rem(lev + step, NR)
                pltpu.make_async_remote_copy(
                    src_ref=radbuf.at[u, to],
                    dst_ref=backbuf.at[pl.ds(u * NMA + 16 * lev, 16)],
                    send_sem=e_send.at[u],
                    recv_sem=b_recv.at[u],
                    device_id=(to, me),
                    device_id_type=MESH,
                ).start()
            pltpu.make_async_copy(
                radbuf.at[u, lev], backbuf.at[pl.ds(u * NMA + 16 * lev, 16)], b_recv.at[u]
            ).start()

    def unpack(buf, out_ref, out_hbm, sem):
        turned[...] = buf[...].astype(F32).reshape(2048, 128)
        for row in range(16):
            packed[pl.ds(row, 128, stride=16), :] = turned[pl.ds(row, 128, stride=16), :].T
        for v in range(6):
            live = masks(v)
            for g, grp in enumerate(OUT_GROUPS):
                half = []
                for h in range(2):
                    spot = (grp * 12 + h * 6 + v) * 16
                    half.append(packed[spot : spot + 16, :])
                for h in range(2):
                    spot = (96 + h * 6 + g) * 16
                    rest = packed[spot : spot + 16, :]
                    cols = slice(768 * h + 128 * v, 768 * h + 128 * v + 128)
                    rows[32 * g : 32 * g + 16, cols] = jnp.where(live[h][0], half[h], 0.0).astype(BF16)
                    other = jnp.where(live[1 - h][0], rest, half[1 - h])
                    rows[32 * g + 16 : 32 * g + 32, cols] = jnp.where(live[h][1], other, 0.0).astype(BF16)
        for w in range(6):
            cols = pl.ds(256 * w, 256)
            out_ref[:, cols] = dot(qback[...], rows[:, cols]).astype(BF16)
            pltpu.make_async_copy(out_ref.at[:, cols], out_hbm.at[:, cols], sem).start()

    for u in range(2):
        rad_derive(u)
    for u in range(2):
        wait_bytes(backbuf.at[pl.ds(u * NMA, NMA)], b_recv.at[u])
    unpack(backbuf, emf_ref, emf_hbm, out_sem.at[0])
    for u in range(2):
        wait_bytes(derbuf.at[pl.ds(u * NMA, NMA)], d_recv.at[u])
    unpack(derbuf, der_ref, der_hbm, out_sem.at[1])

    for u in range(2):
        wait_bytes(sendbuf.at[pl.ds(0, NMA - 1)], f_send.at[u])
        wait_bytes(outbuf.at[pl.ds(0, NMA - 1)], y_send.at[u])

        @pl.when(deriver != lev)
        def _():
            wait_bytes(outbuf.at[0], own_send.at[u])

        wait_bytes(dersend.at[u, pl.ds(0, NR - 1)], d_send.at[u])
        if EMF_HOME[u]:

            @pl.when(deriver != lev)
            def _():
                wait_bytes(outbuf.at[pl.ds(0, NMA - 1)], b_send.at[u])

        else:
            wait_bytes(radbuf.at[u, pl.ds(0, NR - 1)], e_send.at[u])
    wait_bytes(emf_ref, out_sem.at[0])
    wait_bytes(der_ref, out_sem.at[1])


def settle(emf_in, der_in, emf_out, der_out, held, in_sem, out_sem):
    loads, stores = [], []
    for i, (src, dst) in enumerate(((emf_in, emf_out), (der_in, der_out))):
        for part in range(3):
            blk = pl.ds(part * 64, 64)
            loads.append(pltpu.make_async_copy(src.at[blk], held.at[i, blk], in_sem.at[i, part]))
            stores.append(pltpu.make_async_copy(held.at[i, blk], dst.at[blk], out_sem.at[i, part]))
    for load in loads:
        load.start()
    for load, store in zip(loads, stores):
        load.wait()
        store.start()
    for store in stores:
        store.wait()


def per_device(velocity, test_fields, order_slots):
    vel = velocity.reshape(3 * 2 * 16, NTH)
    tst = test_fields.reshape(6 * 2 * 16, NTH)
    fwd, inv = phase_tables()
    vm = pl.BlockSpec(memory_space=pltpu.VMEM)
    sm = pl.BlockSpec(memory_space=pltpu.SMEM)
    hbm = pl.BlockSpec(memory_space=pl.ANY)
    dma = pltpu.SemaphoreType.DMA

    def vmem(*shape, dtype=BF16):
        return pltpu.VMEM(shape, dtype)

    emf, der = pl.pallas_call(
        kernel,
        out_shape=[jax.ShapeDtypeStruct((192, NTH), BF16)] * 2,
        in_specs=[sm, vm] + [hbm] * 6,
        out_specs=[hbm] * 2,
        scratch_shapes=[
            vmem(192, NTH),
            vmem(192, NTH),
            vmem(96, NTH),
            vmem(192, NTH),
            vmem(128, 768),
            vmem(256, 128),
            vmem(2, 2, QUART + 16, PAIRS),
            vmem(2, 2, PAIRS, QUART),
            vmem(2, 2, QUART + 16, PAIRS),
            vmem(2, 2, PAIRS, QUART),
            vmem(2048, 128, dtype=F32),
            vmem(2048, 128, dtype=F32),
            vmem(128, 16, 128),
            vmem(128, 16, 128),
            vmem(PAIRS, PAIRS),
            vmem(PAIRS, PAIRS),
            vmem(PAIRS, 128, dtype=I32),
            vmem(PAIRS, 128, dtype=F32),
            vmem(2, 2, PAIRS, 256),
            vmem(2, 2, QUART, 128),
            vmem(128, 16, 128),
            vmem(128, 16, 128),
            vmem(2, NR, 16, 16, 128),
            vmem(2, NR, 16, 16, 128),
            vmem(128, 16, 128),
            vmem(192, 192),
            vmem(192, 192),
            vmem(192, NTH),
            dma((6,)),
        ]
        + [dma((2,))] * 11
        + [pltpu.SemaphoreType.REGULAR],
        compiler_params=pltpu.CompilerParams(
            collective_id=0, has_side_effects=True, vmem_limit_bytes=60 << 20
        ),
    )(
        order_slots, order_slots.reshape(8, 128), vel, tst,
        jnp.asarray(expand_table()), jnp.asarray(fold_table()), jnp.asarray(fwd), jnp.asarray(inv),
    )
    emf, der = pl.pallas_call(
        settle,
        out_shape=[jax.ShapeDtypeStruct((192, NTH), BF16)] * 2,
        in_specs=[hbm] * 2,
        out_specs=[hbm] * 2,
        scratch_shapes=[vmem(2, 192, NTH), dma((2, 3)), dma((2, 3))],
    )(emf, der)
    shape = (1, 2, 3, 2, 16, NTH)
    return emf.reshape(shape), der.reshape(shape)


def solution(mesh):
    return jax.shard_map(
        per_device,
        mesh=mesh,
        in_specs=(P("rad", None, None, "ma", None), P("rad", None, None, None, "ma", None), P()),
        out_specs=(P("rad", None, None, None, "ma", None), P("rad", None, None, None, "ma", None)),
        check_vma=False,
    )
```

```python
import functools

import jax
import jax.numpy as jnp
import numpy as np
from jax import lax
from jax.experimental import pallas as pl
from jax.experimental.pallas import tpu as pltpu
from jax.sharding import PartitionSpec as P

MESH = pl.DeviceIdType.MESH
M = 1024
NTH = 1536
NPHI = 3072
QUART = NPHI // 4
PAIRS = M // 2
NR = 4
NMA = 64
F32 = jnp.float32
BF16 = jnp.bfloat16
I32 = jnp.int32
PB = 256
EMF_HOME = (False, True)


def cheb_matrix(level_count):
    levels_at = np.arange(level_count)
    points = np.cos(np.pi * levels_at / (level_count - 1))
    weights = np.where((levels_at == 0) | (levels_at == level_count - 1), 2.0, 1.0) * np.where(
        levels_at % 2 == 0, 1.0, -1.0
    )
    identity = np.eye(level_count)
    spread = points[:, None] - points[None, :] + identity
    offdiag = weights[:, None] / weights[None, :] / spread * (1.0 - identity)
    matrix = offdiag - identity * offdiag.sum(axis=1)[:, None]
    return np.asarray(matrix / level_count, dtype=np.float32)


DERIV = cheb_matrix(NR)


def phase_tables():
    r = np.arange(M // 2)
    p = np.arange(QUART + 1)
    fwd = np.zeros((2, 2, QUART + 16, M // 2), np.float32)
    inv = np.zeros((2, 2, M // 2, QUART), np.float32)
    for par, m in enumerate((2 * r, M - 1 - 2 * r)):
        q = (p[:, None] * m[None, :]) % NPHI
        ang = q.astype(np.float32) * np.float32(2.0 * np.pi / NPHI)
        for k, tab in enumerate((np.cos(ang), -np.sin(ang))):
            fwd[par, k, : QUART + 1] = tab
            inv[par, k] = tab[:QUART].T
    inv[:, :, :, 0] *= 0.5
    sign = np.where(r % 2 == 0, 1.0, -1.0)
    fwd[:, :, QUART] = 0.0
    fwd[0, 0, QUART] = sign
    fwd[1, 1, QUART] = sign
    return fwd.astype(jnp.bfloat16), inv.astype(jnp.bfloat16)


def expand_table():
    tab = np.zeros((3, 128, 256), np.float32)
    groups = []
    for f in range(2):
        for g, c in enumerate((1, 2, 0, 1)):
            groups.append((12 * (4 * f + g), c))
    b_first = 128 + 116
    for f in range(2):
        base = 3 + 3 * f
        for g, c in enumerate((2, 0, 1)):
            groups.append((128 + 12 * (4 * f + g), base + c))
        groups.append((b_first if f == 0 else 128 + 36, base + 1))
    for lane0, c in groups:
        for h in range(2):
            for v in range(6):
                lane = lane0 + h * 6 + v
                tab[0, c * 12 + h * 6 + v, lane] = 1
                tab[1, c * 12 + (1 - h) * 6 + v, lane] = 1
                tab[2, 108 + h * 9 + c, lane] = 1
    return np.concatenate(list(tab), axis=1).astype(jnp.bfloat16)


OUT_GROUPS = (0, 1, 2, 4, 5, 6)


def fold_table():
    tab = np.zeros((2, 128, 128), np.float32)
    for g, grp in enumerate(OUT_GROUPS):
        for h in range(2):
            for v in range(6):
                lane = grp * 12 + h * 6 + v
                tab[0, grp * 12 + (1 - h) * 6 + v, lane] = 1
                tab[1, lane, 96 + h * 6 + g] = 1
    return np.concatenate(list(tab), axis=0).astype(jnp.bfloat16)


def dot(a, b):
    return jnp.dot(a, b, preferred_element_type=F32)


def iota(shape, dim):
    return lax.broadcasted_iota(I32, shape, dim)


def onehot(cond):
    return jnp.where(cond, 1.0, 0.0).astype(BF16)


def cross(x):
    a, b = x[:, :128], x[:, 128:]
    return a * b - pltpu.roll(a, 116, 1) * pltpu.roll(b, 12, 1)


def kernel(
    slot_smem, slot_ref, vel_hbm, tst_hbm, exp_hbm, fold_hbm, fwd_hbm, inv_hbm,
    emf_hbm, der_hbm,
    emf_ref, der_ref, vel_ref, tst_ref, exp_ref, fold_ref, fwd_raw, inv_raw, fwd_tab, inv_tab, packed, turned, sendbuf, recvbuf,
    perm, permt, triple, sign, rhs, folded, outbuf, backbuf, radbuf, dersend, derbuf, quse, qback, rows,
    load_sem, f_send, f_recv, b_send, b_recv, y_send, y_recv, d_send, d_recv, own_send, e_send, out_sem, ready,
):
    me = lax.axis_index("ma")
    lev = lax.axis_index("rad")

    barrier = pltpu.get_barrier_semaphore()

    def greet(step, carry):
        pl.semaphore_signal(
            barrier, inc=1, device_id=(lev, lax.rem(me + step, NMA)), device_id_type=MESH
        )
        return carry

    loads = [
        pltpu.make_async_copy(src, dst, load_sem.at[i])
        for i, (src, dst) in enumerate(
            (
                (vel_hbm, vel_ref), (tst_hbm, tst_ref), (fwd_hbm, fwd_raw), (inv_hbm, inv_raw),
                (exp_hbm, exp_ref), (fold_hbm, fold_ref),
            )
        )
    ]
    loads[0].start()
    loads[1].start()
    lax.fori_loop(1, NMA, greet, 0)
    for step in range(1, NR):
        pl.semaphore_signal(barrier, inc=1, device_id=(lax.rem(lev + step, NR), me), device_id_type=MESH)
    for load in loads[2:]:
        load.start()

    firsts = [slot_smem[me * 16 + 2 * i] for i in range(8)]

    def spread(pair, shape):
        out = jnp.full(shape, firsts[7], I32)
        for i in range(7):
            out = jnp.where(pair == i, firsts[i], out)
        return out

    def onehot_rows(dim):
        here = iota((192, 192), dim)
        first = spread(here & 7, (192, 192))
        slot = (here & ~31) + ((here & 8) << 1) + 2 * (here & 7) + (((here >> 4) ^ first) & 1)
        return onehot(slot == iota((192, 192), 1 - dim))

    quse[...] = onehot_rows(0)
    qback[...] = onehot_rows(1)
    lane = iota((16, 128), 1)
    first = spread(iota((16, 128), 0) & 7, (16, 128))
    even = jnp.where((first & 1) == 0, first, (M - 1) - first)
    odd = (M - 1) - even

    def masks(v):
        out = []
        for h in range(2):
            j = 128 * v + lane
            near = (j + 1) if h == 0 else (768 - j)
            out.append((even * NTH <= 2 * M * near, odd * NTH <= 2 * M * near))
        return out

    loads[0].wait()
    loads[1].wait()
    left = {}
    for w in range(3):
        halves = []
        for h in range(2):
            cols = slice(768 * h + 256 * w, 768 * h + 256 * w + 256)
            halves.append(
                (dot(quse[0:96, 0:96], vel_ref[:, cols]), dot(quse[...], tst_ref[:, cols]))
            )
        for vv in range(2):
            v = 2 * w + vv
            live = masks(v)
            for c in range(9):
                xe, xo = [], []
                for h in range(2):
                    src = halves[h][0] if c < 3 else halves[h][1]
                    row = 32 * (c if c < 3 else c - 3)
                    xe.append(src[row : row + 16, 128 * vv : 128 * vv + 128])
                    xo.append(src[row + 16 : row + 32, 128 * vv : 128 * vv + 128])
                for h in range(2):
                    spot = (c * 12 + h * 6 + v) * 16
                    packed[spot : spot + 16, :] = jnp.where(live[h][0], xe[h], xo[1 - h])
                    rest = jnp.where(live[h][1] & live[1 - h][0], xo[h], 0.0)
                    left[h, c] = rest if v == 0 else left[h, c] + rest
    for h in range(2):
        for c in range(9):
            spot = (108 + h * 9 + c) * 16
            packed[spot : spot + 16, :] = left[h, c]
    packed[126 * 16 : 128 * 16, :] = jnp.zeros((32, 128), F32)
    for row in range(16):
        turned[pl.ds(row, 128, stride=16), :] = packed[pl.ds(row, 128, stride=16), :].T
    sendbuf[...] = turned[...].astype(BF16).reshape(128, 16, 128)

    pl.semaphore_wait(barrier, NMA - 1 + NR - 1)
    for step in range(1, NR):
        pl.semaphore_signal(ready, inc=1, device_id=(lax.rem(lev + step, NR), me), device_id_type=MESH)

    def all_to_all(src, dst, ssem, rsem, u):
        def one(step, carry):
            to = lax.rem(me + step, NMA)
            pltpu.make_async_remote_copy(
                src_ref=src.at[u * NMA + to],
                dst_ref=dst.at[u * NMA + me],
                send_sem=ssem.at[u],
                recv_sem=rsem.at[u],
                device_id=(lev, to),
                device_id_type=MESH,
            ).start()
            return carry

        pltpu.make_async_copy(src.at[u * NMA + me], dst.at[u * NMA + me], rsem.at[u]).start()
        lax.fori_loop(1, NMA, one, 0)

    deriver = me // 16
    place = lax.rem(me, 16)

    def to_deriver(u, b):
        def one(step, carry):
            to = 16 * b + lax.rem(me + step, 16)

            @pl.when(to != me)
            def _():
                pltpu.make_async_remote_copy(
                    src_ref=outbuf.at[u * NMA + to],
                    dst_ref=radbuf.at[u, lev, place],
                    send_sem=y_send.at[u],
                    recv_sem=y_recv.at[u],
                    device_id=(deriver, to),
                    device_id_type=MESH,
                ).start()

            return carry

        lax.fori_loop(0, 16, one, 0)

    def own_to_deriver(u):
        @pl.when(deriver == lev)
        def _():
            pltpu.make_async_copy(outbuf.at[u * NMA + me], radbuf.at[u, lev, place], y_recv.at[u]).start()

        @pl.when(deriver != lev)
        def _():
            pltpu.make_async_remote_copy(
                src_ref=outbuf.at[u * NMA + me],
                dst_ref=radbuf.at[u, lev, place],
                send_sem=own_send.at[u],
                recv_sem=y_recv.at[u],
                device_id=(deriver, me),
                device_id_type=MESH,
            ).start()

    def wait_bytes(ref, sem):
        pltpu.make_async_copy(ref, ref, sem).wait()

    for u in range(2):
        all_to_all(sendbuf, recvbuf, f_send, f_recv, u)

    slots = slot_ref[...]
    rank = jnp.where((slots & 1) == 0, slots, (M - 1) - slots) >> 1
    high = (rank >> 4).astype(F32).astype(BF16)
    low = (rank & 15).astype(F32).astype(BF16)
    at_row, at_lane = iota((128, 128), 0), iota((128, 128), 1)
    parts = []
    for side in range(2):
        pick = onehot(at_row == 2 * (at_lane - 64 * side))
        parts.append(dot(high, pick) * 16.0 + dot(low, pick))
    keys = jnp.concatenate([parts[0][2 * b : 2 * b + 1] + parts[1][2 * b + 1 : 2 * b + 2] for b in range(4)] * 2, axis=0)
    keys_t = keys.T
    for b in range(4):
        blk = slice(128 * b, 128 * b + 128)
        perm[:, blk] = onehot(keys[b : b + 1, :] == iota((PAIRS, 128), 0).astype(F32))
        column = keys_t[:, b : b + 1]
        permt[blk, :] = onehot(column == iota((128, PAIRS), 1).astype(F32))
        wide = jnp.broadcast_to(column, (128, 128)).astype(I32)
        triple[blk, :] = 3 * wide
        sign[blk, :] = (1 - 2 * (wide & 1)).astype(F32)

    for load in loads[2:]:
        load.wait()

    def build(i, carry):
        for par in range(2):
            for k in range(2):
                spot = pl.ds(pl.multiple_of(i * 256, 256), 256)
                fwd_tab[par, k, spot, :] = dot(fwd_raw[par, k, spot, :], perm[...]).astype(BF16)
                inv_tab[par, k, :, spot] = dot(permt[...], inv_raw[par, k, :, spot]).astype(BF16)
        return carry

    lax.fori_loop(0, QUART // 256, build, 0)
    for par in range(2):
        for k in range(2):
            last = slice(QUART, QUART + 16)
            fwd_tab[par, k, last, :] = dot(fwd_raw[par, k, last, :], perm[...]).astype(BF16)

    def near_of(lane_id, u):
        l12 = jnp.where(lane_id >= 116, lane_id - 116, lax.rem(lane_id, 12))
        h = l12 >= 6
        v = jnp.where(h, l12 - 6, l12)
        j = 128 * v + 64 * u + me
        return jnp.where(h, 768 - j, j + 1)

    scale = NPHI ** (-0.5)

    for u in range(2):
        lane1 = iota((1, 128), 1)
        near = near_of(lane1, u)
        main = lane1 < 96
        own_top, far_top, odd_low = 2 * near, 1538 - 2 * near, 1535 - 2 * near
        wait_bytes(recvbuf.at[pl.ds(u * NMA, NMA)], f_recv.at[u])
        for b in range(4):
            blk = slice(128 * b, 128 * b + 128)
            got = recvbuf[u * NMA + 16 * b : u * NMA + 16 * b + 16].reshape(256, 128)
            wide = dot(got, exp_ref[...]).reshape(16, 2, 8, 768)
            tri = triple[blk, :]
            own_live = tri <= own_top
            far_live = tri <= far_top
            odd_live = tri >= odd_low
            for k in range(2):
                part = wide[:, k].reshape(128, 768)
                for t in range(2):
                    cols = slice(128 * t, 128 * t + 128)
                    same, swap, rest = (part[:, 256 * i + 128 * t : 256 * i + 128 * t + 128] for i in range(3))
                    rhs[0, k, blk, cols] = jnp.where(own_live, same, 0.0).astype(BF16)
                    other = jnp.where(far_live, rest, swap)
                    rhs[1, k, blk, cols] = jnp.where(odd_live, other, 0.0).astype(BF16)

        def longitudes(i, carry):
            spot = pl.ds(pl.multiple_of(i * PB, PB), PB)
            ce, se, co, so = (
                dot(fwd_tab[par, k, spot, :], rhs[par, k]) for par in range(2) for k in range(2)
            )
            ve, vo = ce + se, co + so
            me_, mo = ce - se, so - co
            e1, e2 = cross(ve + vo), cross(ve - vo)
            e3, e4 = cross(me_ + mo), cross(me_ - mo)
            us, ws, um, wm = e1 + e2, e1 - e2, e3 + e4, e3 - e4
            folded[0, 0, spot, :] = (us + um).astype(BF16)
            folded[0, 1, spot, :] = (us - um).astype(BF16)
            folded[1, 0, spot, :] = (ws - wm).astype(BF16)
            folded[1, 1, spot, :] = (ws + wm).astype(BF16)
            return carry

        lax.fori_loop(0, QUART // PB, longitudes, 0, unroll=True)
        last = slice(QUART, QUART + 16)
        ve, vo = (
            dot(fwd_tab[par, 0, last, :], rhs[par, 0]) + dot(fwd_tab[par, 1, last, :], rhs[par, 1])
            for par in range(2)
        )
        e1, e2 = cross(ve + vo), cross(ve - vo)
        quarter = ((e1 + e2)[0:1], (e1 - e2)[0:1])

        for b in range(4):
            blk = slice(128 * b, 128 * b + 128)
            tri = triple[blk, :]
            own_live = (tri <= own_top) & main
            both_live = (tri >= odd_low) & (tri <= far_top) & main
            out = []
            for k in range(2):
                se = dot(inv_tab[0, k, blk, :], folded[0, k])
                so = dot(inv_tab[1, k, blk, :], folded[1, k])
                if k == 0:
                    se = se + sign[blk, :] * quarter[0]
                else:
                    so = so + sign[blk, :] * quarter[1]
                so = so * scale
                rest = jnp.where(both_live, so, 0.0)
                moved = dot(jnp.concatenate([so, rest], axis=1).astype(BF16), fold_ref[...])
                out.append(jnp.where(own_live, se * scale, moved).reshape(16, 1, 8, 128))
            outbuf[u * NMA + 16 * b : u * NMA + 16 * b + 16] = (
                jnp.concatenate(out, axis=1).reshape(16, 16, 128).astype(BF16)
            )
            if u == 0 and b == 0:
                pl.semaphore_wait(ready, NR - 1)
            to_deriver(u, b)
        own_to_deriver(u)
        if EMF_HOME[u]:
            all_to_all(outbuf, backbuf, b_send, b_recv, u)

    def rad_derive(u):
        wait_bytes(radbuf.at[u], y_recv.at[u])
        vals = [radbuf[u, k].astype(F32) for k in range(NR)]
        for i in range(NR):
            acc = vals[0] * float(DERIV[i, 0])
            for k in range(1, NR):
                acc = acc + vals[k] * float(DERIV[i, k])
            dersend[u, i] = acc.astype(BF16)
        for step in range(1, NR):
            to = lax.rem(lev + step, NR)
            pltpu.make_async_remote_copy(
                src_ref=dersend.at[u, to],
                dst_ref=derbuf.at[pl.ds(u * NMA + 16 * lev, 16)],
                send_sem=d_send.at[u],
                recv_sem=d_recv.at[u],
                device_id=(to, me),
                device_id_type=MESH,
            ).start()
        pltpu.make_async_copy(
            dersend.at[u, lev], derbuf.at[pl.ds(u * NMA + 16 * lev, 16)], d_recv.at[u]
        ).start()
        if not EMF_HOME[u]:
            for step in range(1, NR):
                to = lax.rem(lev + step, NR)
                pltpu.make_async_remote_copy(
                    src_ref=radbuf.at[u, to],
                    dst_ref=backbuf.at[pl.ds(u * NMA + 16 * lev, 16)],
                    send_sem=e_send.at[u],
                    recv_sem=b_recv.at[u],
                    device_id=(to, me),
                    device_id_type=MESH,
                ).start()
            pltpu.make_async_copy(
                radbuf.at[u, lev], backbuf.at[pl.ds(u * NMA + 16 * lev, 16)], b_recv.at[u]
            ).start()

    def unpack(buf, out_ref, out_hbm, sem):
        turned[...] = buf[...].astype(F32).reshape(2048, 128)
        for row in range(16):
            packed[pl.ds(row, 128, stride=16), :] = turned[pl.ds(row, 128, stride=16), :].T
        for v in range(6):
            live = masks(v)
            for g, grp in enumerate(OUT_GROUPS):
                half = []
                for h in range(2):
                    spot = (grp * 12 + h * 6 + v) * 16
                    half.append(packed[spot : spot + 16, :])
                for h in range(2):
                    spot = (96 + h * 6 + g) * 16
                    rest = packed[spot : spot + 16, :]
                    cols = slice(768 * h + 128 * v, 768 * h + 128 * v + 128)
                    rows[32 * g : 32 * g + 16, cols] = jnp.where(live[h][0], half[h], 0.0).astype(BF16)
                    other = jnp.where(live[1 - h][0], rest, half[1 - h])
                    rows[32 * g + 16 : 32 * g + 32, cols] = jnp.where(live[h][1], other, 0.0).astype(BF16)
        for w in range(6):
            cols = pl.ds(256 * w, 256)
            out_ref[:, cols] = dot(qback[...], rows[:, cols]).astype(BF16)
            pltpu.make_async_copy(out_ref.at[:, cols], out_hbm.at[:, cols], sem).start()

    for u in range(2):
        rad_derive(u)
    for u in range(2):
        wait_bytes(backbuf.at[pl.ds(u * NMA, NMA)], b_recv.at[u])
    unpack(backbuf, emf_ref, emf_hbm, out_sem.at[0])
    for u in range(2):
        wait_bytes(derbuf.at[pl.ds(u * NMA, NMA)], d_recv.at[u])
    unpack(derbuf, der_ref, der_hbm, out_sem.at[1])

    for u in range(2):
        wait_bytes(sendbuf.at[pl.ds(0, NMA - 1)], f_send.at[u])
        wait_bytes(outbuf.at[pl.ds(0, NMA - 1)], y_send.at[u])

        @pl.when(deriver != lev)
        def _():
            wait_bytes(outbuf.at[0], own_send.at[u])

        wait_bytes(dersend.at[u, pl.ds(0, NR - 1)], d_send.at[u])
        if EMF_HOME[u]:
            wait_bytes(outbuf.at[pl.ds(0, NMA - 1)], b_send.at[u])
        else:
            wait_bytes(radbuf.at[u, pl.ds(0, NR - 1)], e_send.at[u])
    wait_bytes(emf_ref, out_sem.at[0])
    wait_bytes(der_ref, out_sem.at[1])


def settle(emf_in, der_in, emf_out, der_out, held, in_sem, out_sem):
    loads, stores = [], []
    for i, (src, dst) in enumerate(((emf_in, emf_out), (der_in, der_out))):
        for part in range(3):
            blk = pl.ds(part * 64, 64)
            loads.append(pltpu.make_async_copy(src.at[blk], held.at[i, blk], in_sem.at[i, part]))
            stores.append(pltpu.make_async_copy(held.at[i, blk], dst.at[blk], out_sem.at[i, part]))
    for load in loads:
        load.start()
    for load, store in zip(loads, stores):
        load.wait()
        store.start()
    for store in stores:
        store.wait()


def per_device(velocity, test_fields, order_slots):
    vel = velocity.reshape(3 * 2 * 16, NTH)
    tst = test_fields.reshape(6 * 2 * 16, NTH)
    fwd, inv = phase_tables()
    vm = pl.BlockSpec(memory_space=pltpu.VMEM)
    sm = pl.BlockSpec(memory_space=pltpu.SMEM)
    hbm = pl.BlockSpec(memory_space=pl.ANY)
    dma = pltpu.SemaphoreType.DMA

    def vmem(*shape, dtype=BF16):
        return pltpu.VMEM(shape, dtype)

    emf, der = pl.pallas_call(
        kernel,
        out_shape=[jax.ShapeDtypeStruct((192, NTH), BF16)] * 2,
        in_specs=[sm, vm] + [hbm] * 6,
        out_specs=[hbm] * 2,
        scratch_shapes=[
            vmem(192, NTH),
            vmem(192, NTH),
            vmem(96, NTH),
            vmem(192, NTH),
            vmem(128, 768),
            vmem(256, 128),
            vmem(2, 2, QUART + 16, PAIRS),
            vmem(2, 2, PAIRS, QUART),
            vmem(2, 2, QUART + 16, PAIRS),
            vmem(2, 2, PAIRS, QUART),
            vmem(2048, 128, dtype=F32),
            vmem(2048, 128, dtype=F32),
            vmem(128, 16, 128),
            vmem(128, 16, 128),
            vmem(PAIRS, PAIRS),
            vmem(PAIRS, PAIRS),
            vmem(PAIRS, 128, dtype=I32),
            vmem(PAIRS, 128, dtype=F32),
            vmem(2, 2, PAIRS, 256),
            vmem(2, 2, QUART, 128),
            vmem(128, 16, 128),
            vmem(128, 16, 128),
            vmem(2, NR, 16, 16, 128),
            vmem(2, NR, 16, 16, 128),
            vmem(128, 16, 128),
            vmem(192, 192),
            vmem(192, 192),
            vmem(192, NTH),
            dma((6,)),
        ]
        + [dma((2,))] * 11
        + [pltpu.SemaphoreType.REGULAR],
        compiler_params=pltpu.CompilerParams(
            collective_id=0, has_side_effects=True, vmem_limit_bytes=60 << 20
        ),
    )(
        order_slots, order_slots.reshape(8, 128), vel, tst,
        jnp.asarray(expand_table()), jnp.asarray(fold_table()), jnp.asarray(fwd), jnp.asarray(inv),
    )
    emf, der = pl.pallas_call(
        settle,
        out_shape=[jax.ShapeDtypeStruct((192, NTH), BF16)] * 2,
        in_specs=[hbm] * 2,
        out_specs=[hbm] * 2,
        scratch_shapes=[vmem(2, 192, NTH), dma((2, 3)), dma((2, 3))],
    )(emf, der)
    shape = (1, 2, 3, 2, 16, NTH)
    return emf.reshape(shape), der.reshape(shape)


def solution(mesh):
    return jax.shard_map(
        per_device,
        mesh=mesh,
        in_specs=(P("rad", None, None, "ma", None), P("rad", None, None, None, "ma", None), P()),
        out_specs=(P("rad", None, None, None, "ma", None), P("rad", None, None, None, "ma", None)),
        check_vma=False,
    )
```
